256 devices in a mesh: row: 4 (over z_hi), col: 64 (over y, x, z_lo, core).
Axes of the slice: x: 4, y: 4, z: 8 (z_hi: 4, z_lo: 2; z = z_hi * 2 + z_lo), core: 2. Of those that a mesh axis runs over, the one named last changes fastest.
Arguments:
- grm_tiles: bfloat16 [1024, 1024, 1024], P(('row', 'col')), as said below
- tile_row: int32 [1024], P(('row', 'col')), may hold values from 0 to 7, as said below
- tile_col: int32 [1024], P(('row', 'col')), may hold values from -1 to 127, as said below
- panel: bfloat16 [131072, 128], P('col'), may hold values from -6 to 6
Outputs:
- y_rows: float32 [8192, 128], P(('row', 'col'))
- y_cols: float32 [131072, 128], P('col')
The draws below stay inside these ranges and needn't reach their ends.
Inputs may be any that keep to these rules, and one draw needn't show every extreme that they name: The slots of the device with index r on row and c on col hold slab row tiles r * 2 to r * 2 + 1 and column tiles c * 2 to c * 2 + 1; every pair of these with column tile <= 120 + row tile stands in exactly one of that device's slots, in an order drawn from the seed; in the other slots tile_col is -1 and tile_row still names a row tile of the device. `tile_col`: as for tile_row. `grm_tiles`: entries of a diagonal tile above its diagonal are not used.
All inputs are finite; a program needn't handle non-finite values.
Results may differ from the reference program's by a relative error of at most 0.0003.
Values may be sent and summed in bfloat16 or wider, within the bound.
No kernel may reach another device: no remote copies, remote signals or barrier semaphores. Data moves between devices by JAX's collectives and lax.ppermute only.
A program may use at most 64 MiB of HBM per device.

```python
import jax
import jax.numpy as jnp
from jax import lax

B = 1024
K = 128
RT_DEV = 2
CTD = 2
RT = 8
START = 120
TILES_DEV = 4
SLOTS = 1024
PEOPLE = 131072
N_ROW = 4
N_COL = 64


def slot_order(device_key):
    return jax.random.permutation(device_key, TILES_DEV)


def slot_layout(key):
    devices = N_ROW * N_COL
    device_keys = jax.random.split(key, devices)
    positions = jax.vmap(slot_order)(device_keys)
    device = jnp.arange(devices, dtype=jnp.int32)[:, None]
    row_tile = device // N_COL * RT_DEV + positions // CTD
    column = device % N_COL * CTD + positions % CTD
    column = jnp.where(column <= START + row_tile, column, -1)
    return (row_tile.reshape(-1).astype(jnp.int32), column.reshape(-1).astype(jnp.int32))


def draw_tile_row(key, part):
    row_tile, column = slot_layout(key)
    return row_tile


def draw_tile_col(key, part):
    row_tile, column = slot_layout(key)
    return column


def draw_grm_tiles(key, part):
    row_tile, column = slot_layout(key)
    key = jax.random.fold_in(key, 7)
    entry_key, self_key = jax.random.split(key)
    scale = PEOPLE ** (-0.5)
    values = jax.random.normal(entry_key, (SLOTS, B, B), jnp.float32) * scale
    selfrel = 1.0 + 0.5 * jax.random.uniform(self_key, (SLOTS, B, B), jnp.float32)
    diagonal_tile = (column == START + row_tile)[:, None, None]
    within = (jnp.arange(B)[:, None] == jnp.arange(B)[None, :])[None, :, :]
    values = jnp.where(jnp.logical_and(diagonal_tile, within), selfrel, values)
    return values.astype(jnp.bfloat16)


def level_of(stream_key, shape, cuts, least, largest):
    gain, own = 1.0, jax.random.fold_in(stream_key, 6)
    for dim, blocks in cuts:
        draws = jnp.exp(jax.random.uniform(jax.random.fold_in(own, dim), (blocks,), jnp.float32, least / len(cuts), largest / len(cuts)))
        gain = gain * jnp.repeat(draws, shape[dim] // blocks).reshape([-1 if axis == dim else 1 for axis in range(len(shape))])
    return gain


def bell_draw(stream_key, shape, spread, most, pieces=(), kind=jnp.bfloat16):
    level = level_of(stream_key, shape, pieces, -0.22, 0.18) if pieces else 1.0
    array = jax.random.normal(stream_key, shape, jnp.float32) * spread * level
    return jnp.minimum(jnp.maximum(array, -most), most).astype(kind)


def setup_inputs(seed: int = 0) -> dict:
    keys = jax.random.split(jax.random.key(seed), 5)
    return {
        "grm_tiles": draw_grm_tiles(jax.random.fold_in(keys[4], 71), 0),
        "tile_row": draw_tile_row(jax.random.fold_in(keys[4], 71), 0),
        "tile_col": draw_tile_col(jax.random.fold_in(keys[4], 71), 0),
        "panel": bell_draw(keys[3], (PEOPLE, K), 1.0, 6.0, ((0, 64),)),
    }


def complete_tile(tile, diagonal_tile):
    size = tile.shape[0]
    lower_mask = lax.broadcasted_iota(jnp.int32, (size, size), 0) >= lax.broadcasted_iota(jnp.int32, (size, size), 1)
    return jnp.where(diagonal_tile, jnp.where(lower_mask, tile, tile.T), tile)


def reference(grm_tiles, tile_row, tile_col, panel):
    row_start = jnp.zeros((RT * B, K), jnp.float32)
    col_start = jnp.zeros((PEOPLE, K), jnp.float32)

    def one_slot(carry, inputs):
        rows_sum, cols_sum = carry
        tile, row_tile, col_tile = inputs
        present = col_tile >= 0
        safe_col = jnp.maximum(col_tile, 0).astype(jnp.int32)
        diagonal_tile = col_tile == START + row_tile
        source = lax.dynamic_slice_in_dim(panel, (safe_col * B).astype(jnp.int32), B, 0)
        product = jnp.dot(complete_tile(tile, diagonal_tile), source, preferred_element_type=jnp.float32)
        product = jnp.where(present, product, jnp.zeros_like(product))
        place = (row_tile * B).astype(jnp.int32)
        current = lax.dynamic_slice_in_dim(rows_sum, place, B, 0)
        rows_sum = lax.dynamic_update_slice_in_dim(rows_sum, current + product, place, 0)
        slab_rows = lax.dynamic_slice_in_dim(panel, ((START + row_tile) * B).astype(jnp.int32), B, 0)
        mirror = lax.dot_general(tile, slab_rows, (((0,), (0,)), ((), ())), preferred_element_type=jnp.float32)
        keep = jnp.logical_and(present, col_tile < START + row_tile)
        mirror = jnp.where(keep, mirror, jnp.zeros_like(mirror))
        target = (safe_col * B).astype(jnp.int32)
        current = lax.dynamic_slice_in_dim(cols_sum, target, B, 0)
        cols_sum = lax.dynamic_update_slice_in_dim(cols_sum, current + mirror, target, 0)
        return (rows_sum, cols_sum), None

    (y_rows, y_cols), unused = lax.scan(one_slot, (row_start, col_start), (grm_tiles, tile_row, tile_col))
    return y_rows, y_cols
```

```python
import functools

import jax
import jax.numpy as jnp
from jax import lax
from jax.experimental import pallas as pl
from jax.experimental.pallas import tpu as pltpu
from jax.sharding import PartitionSpec as P

RT_DEV = 2
CTD = 2
STEPS = 2
MIB = 1024 * 1024
PAD = 16
SITES = 16
PLANES = 4
LINE = 4
BF16_MOST = 3.3895313892515355e38


def site_at(place):
    return place % LINE * LINE + place // LINE


def place_of(info, index, depth, width):
    slot = index // STEPS
    part = index % STEPS
    local_row = info[0, slot]
    local_col = info[1, slot]
    first = pl.multiple_of(local_row * width + part * depth, depth)
    rows = pl.ds(first, depth)
    cols = pl.ds(pl.multiple_of(local_col * width, width), width)
    piece = pl.ds(pl.multiple_of(part * depth, depth), depth)
    return slot, part, rows, cols, piece


def fetch_of(info, tiles_ref, held, sems):
    slots, width, _ = held.shape
    depth = width // STEPS

    def fetch(index):
        slot, part, rows, cols, piece = place_of(info, index, depth, width)
        return pltpu.make_async_copy(
            tiles_ref.at[slot, piece], held.at[slot, piece], sems.at[index]
        )

    return fetch


def row_kernel(info, tiles_ref, panel_ref, keep_ref, send_ref, total, held, sems):
    slots, width, _ = held.shape
    depth = width // STEPS
    fetch = fetch_of(info, tiles_ref, held, sems)
    for index in range(slots * STEPS):
        fetch(index).start()
    total[...] = jnp.zeros_like(total)

    @pl.loop(0, slots * STEPS)
    def _(index):
        slot, part, rows, cols, piece = place_of(info, index, depth, width)
        kind = info[2, slot]
        fetch(index).wait()

        @pl.when(kind == 1)
        def _():
            total[rows, :] += jnp.dot(
                held[slot, piece, :], panel_ref[cols, :], preferred_element_type=jnp.float32
            )

        @pl.when(kind == 2)
        def _():
            row_ids = lax.broadcasted_iota(jnp.int32, (depth, width), 0) + part * depth
            col_ids = lax.broadcasted_iota(jnp.int32, (depth, width), 1)
            tile = held[slot, piece, :].astype(jnp.float32)
            lower = jnp.where(row_ids >= col_ids, tile, 0.0).astype(jnp.bfloat16)
            strict = jnp.where(row_ids > col_ids, tile, 0.0).astype(jnp.bfloat16)
            total[rows, :] += jnp.dot(lower, panel_ref[cols, :], preferred_element_type=jnp.float32)
            own = pl.ds(pl.multiple_of(info[1, slot] * width + part * depth, depth), depth)
            whole = pl.ds(pl.multiple_of(info[0, slot] * width, width), width)
            total[whole, :] += lax.dot_general(
                panel_ref[own, :], strict, (((0,), (0,)), ((), ())),
                preferred_element_type=jnp.float32,
            ).T

    core = info[4, 0]
    depth_z = info[4, 1]
    share = total.shape[0] // (SITES * PLANES)
    for ref, which in ((keep_ref, core), (send_ref, 1 - core)):
        for step, chip in enumerate((depth_z, 1 - depth_z)):
            for place in range(SITES):
                site = site_at(place)
                source = pl.multiple_of((site * PLANES + chip * 2 + which) * share, share)
                target = (step * SITES + place) * share
                ref[target : target + share, :] = total[pl.ds(source, share), :]


def add_kernel(keep_ref, got_ref, mine_ref, send_ref):
    size = mine_ref.shape[0]
    mine_ref[...] = keep_ref[:size, :] + got_ref[:size, :]
    encode(keep_ref[size:, :] + got_ref[size:, :], send_ref)


def sum_of(refs):
    total = refs[0][...].astype(jnp.float32)
    for ref in refs[1:]:
        total += ref[...].astype(jnp.float32)
    return total.astype(refs[0].dtype)


def strip_kernel(home, bits, panel_ref, got1_ref, got2_ref, got3_ref, after_ref, *out_refs):
    del after_ref
    rows = got1_ref.shape[0]
    own = panel_ref[home * rows : (home + 1) * rows, :].astype(jnp.float32)
    own = jnp.where(bits[4] == 1, own, 0.0)
    rest = got1_ref[...].astype(jnp.float32) + got2_ref[...].astype(jnp.float32)
    strip = (own + rest + got3_ref[...].astype(jnp.float32)).astype(jnp.bfloat16)
    size = rows // LINE
    for index, out_ref in enumerate(out_refs):
        out_ref[...] = strip[index * size : (index + 1) * size]


def sum_kernel(*refs):
    refs[-1][...] = sum_of(refs[:-1])


def pack_kernel(mine_ref, got_ref, piece_ref, got1_ref, got2_ref, got3_ref, out_ref):
    sites = out_ref.shape[0]
    size = piece_ref.shape[0]
    share = mine_ref.shape[0] // sites
    piece = sum_of((piece_ref, got1_ref, got2_ref, got3_ref))
    sums = mine_ref[...] + decode(got_ref)
    high = jnp.clip(sums, -BF16_MOST, BF16_MOST).astype(jnp.bfloat16)
    low = (sums - high.astype(jnp.float32)).astype(jnp.bfloat16)
    for site in range(sites):
        out_ref[site, :size, :] = piece
        out_ref[site, size : size + share, :] = high[site * share : (site + 1) * share]
        out_ref[site, size + share :, :] = low[site * share : (site + 1) * share]


def block_rows(size):
    return min(128, size)


def encode(value, out_ref):
    size = value.shape[0]
    block = block_rows(size)
    lanes = value.shape[1]
    powers = []
    for start in range(0, size, block):
        part = value[start : start + block]
        most = jnp.max(jnp.abs(part), axis=0, keepdims=True)
        power = 15.0 - jnp.maximum(jnp.ceil(jnp.log2(most)), -126.0)
        half = jnp.floor(power * 0.5)
        scaled = part * jnp.exp2(half) * jnp.exp2(power - half)
        whole = jnp.clip(jnp.round(scaled), -32767.0, 32767.0)
        out_ref[start : start + block, :] = whole.astype(jnp.int32).astype(jnp.int16)
        powers.append(power)
    powers.append(jnp.zeros((PAD - len(powers), lanes), jnp.float32))
    tail = jnp.concatenate(powers, axis=0)
    out_ref[size:, :] = tail.astype(jnp.int32).astype(jnp.int16)


def decode(ref):
    size = ref.shape[0] - PAD
    block = block_rows(size)
    tail = ref[size:, :].astype(jnp.int32).astype(jnp.float32)
    parts = []
    for index in range(size // block):
        power = tail[index : index + 1]
        half = jnp.floor(power * 0.5)
        part = ref[index * block : (index + 1) * block, :].astype(jnp.int32).astype(jnp.float32)
        parts.append(part * jnp.exp2(-half) * jnp.exp2(half - power))
    return jnp.concatenate(parts, axis=0)


def col_kernel(
    info, tiles_ref, slab_ref, rows_ref, keep_ref, send0_ref, send1_ref, total, result, held, sems
):
    slots, width, _ = held.shape
    depth = width // STEPS
    size, share = slab_ref.shape[1], rows_ref.shape[0]
    size = size - 2 * share
    count = depth // size
    fetch = fetch_of(info, tiles_ref, held, sems)
    for index in range(slots * STEPS):
        fetch(index).start()
    total[...] = jnp.zeros_like(total)
    sums = jnp.zeros(rows_ref.shape, jnp.float32)
    for site in range(slab_ref.shape[0]):
        sums += slab_ref[site, size : size + share, :].astype(jnp.float32)
        sums += slab_ref[site, size + share :, :].astype(jnp.float32)
    rows_ref[...] = sums

    @pl.loop(0, slots * STEPS)
    def _(index):
        slot, part, rows, cols, piece = place_of(info, index, depth, width)
        fetch(index).wait()

        @pl.when(info[2, slot] == 1)
        def _():
            first = (info[0, slot] * STEPS + part) * count
            source = slab_ref[pl.ds(first, count), :size, :].reshape(depth, slab_ref.shape[2])
            total[:, cols] += lax.dot_general(
                source, held[slot, piece, :], (((0,), (0,)), ((), ())),
                preferred_element_type=jnp.float32,
            )

    result[...] = total[...].T
    half = width // 2
    for index, send_ref in enumerate((send0_ref, send1_ref)):
        bit = info[3, index]
        mine = pl.multiple_of(index * width + bit * half, half)
        other = pl.multiple_of(index * width + (1 - bit) * half, half)
        keep_ref[index] = result[pl.ds(mine, half), :]
        encode(result[pl.ds(other, half), :], send_ref)


def first_kernel(index, keep_ref, got_ref, out_ref):
    encode(keep_ref[index] + decode(got_ref), out_ref)


def second_kernel(own_ref, got_ref, out_ref):
    encode(decode(own_ref) + decode(got_ref), out_ref)


def place_kernel(index, bits, own_ref, got_ref, *refs):
    out_ref, held, sem = refs[-3:]
    size = own_ref.shape[0] - PAD
    mine = pl.multiple_of(bits[index] * size, size)
    other = pl.multiple_of((1 - bits[index]) * size, size)
    held[pl.ds(mine, size), :] = decode(own_ref)
    held[pl.ds(other, size), :] = decode(got_ref)
    copy = pltpu.make_async_copy(held, out_ref.at[pl.ds(index * 2 * size, 2 * size)], sem)
    copy.start()
    copy.wait()


VMEM = pl.BlockSpec(memory_space=pltpu.VMEM)
SMEM = pl.BlockSpec(memory_space=pltpu.SMEM)
HBM = pl.BlockSpec(memory_space=pltpu.HBM)
ANY = pl.BlockSpec(memory_space=pl.ANY)


def limit(size):
    return pltpu.CompilerParams(vmem_limit_bytes=size * MIB)


def small_call(kernel, outs, *args, scalars=0, after=None):
    specs = [SMEM] * scalars + [VMEM] * (len(args) - scalars)
    if after is not None:
        specs, args = specs + [ANY], args + (after,)
    return pl.pallas_call(
        kernel, in_specs=specs, out_specs=[VMEM] * len(outs), out_shape=outs, compiler_params=limit(6)
    )(*args)


def place_half(index, bits, own, got, result):
    size, lanes = own.shape[0] - PAD, own.shape[1]
    args = (bits, own, got) + (() if result is None else (result,))
    return pl.pallas_call(
        functools.partial(place_kernel, index),
        in_specs=[SMEM, VMEM, VMEM] + [HBM] * (len(args) - 3),
        out_specs=HBM,
        out_shape=floats(4 * size, lanes),
        scratch_shapes=[pltpu.VMEM((2 * size, lanes), jnp.float32), pltpu.SemaphoreType.DMA],
        input_output_aliases={} if result is None else {3: 0},
        compiler_params=limit(6),
    )(*args)


def tile_cost(shape, lanes):
    slots, width, _ = shape
    return pl.CostEstimate(
        flops=2 * slots * width * width * lanes,
        bytes_accessed=2 * slots * width * width + 2 * MIB,
        transcendentals=0,
    )


def floats(*shape):
    return jax.ShapeDtypeStruct(shape, jnp.float32)


def coded(size, lanes):
    return jax.ShapeDtypeStruct((size + PAD, lanes), jnp.int16)


def tile_scratch(grm_tiles):
    return [
        pltpu.VMEM(grm_tiles.shape, grm_tiles.dtype),
        pltpu.SemaphoreType.DMA((grm_tiles.shape[0] * STEPS,)),
    ]


def row_products(info, grm_tiles, panel):
    slots, width, _ = grm_tiles.shape
    lanes = panel.shape[1]
    rows = RT_DEV * width
    return pl.pallas_call(
        row_kernel,
        in_specs=[SMEM, HBM, VMEM],
        out_specs=[VMEM, VMEM],
        out_shape=[floats(rows // 2, lanes), floats(rows // 2, lanes)],
        scratch_shapes=[pltpu.VMEM((rows, lanes), jnp.float32)] + tile_scratch(grm_tiles),
        compiler_params=limit(24),
        cost_estimate=tile_cost(grm_tiles.shape, lanes),
    )(info, grm_tiles, panel)


def col_products(info, grm_tiles, packed, share):
    slots, width, _ = grm_tiles.shape
    lanes = packed.shape[2]
    half = width // 2
    return pl.pallas_call(
        col_kernel,
        in_specs=[SMEM, HBM, VMEM],
        out_specs=[VMEM] * 4,
        out_shape=[floats(share, lanes), floats(2, half, lanes), coded(half, lanes), coded(half, lanes)],
        scratch_shapes=[
            pltpu.VMEM((lanes, CTD * width), jnp.float32),
            pltpu.VMEM((CTD * width, lanes), jnp.float32),
        ]
        + tile_scratch(grm_tiles),
        compiler_params=limit(24),
        cost_estimate=tile_cost(grm_tiles.shape, lanes),
    )(info, grm_tiles, packed)


def swap(value, axis, flip):
    return lax.ppermute(value, axis, [(k, k ^ flip) for k in range(lax.axis_size(axis))])


def sum_over_row(bits, keep, sends):
    size, lanes = keep.shape[1:]
    outs = [coded(size, lanes)]
    flips = [(1, 3, 1), (3, 1, 3)]
    gots = [swap(send, "row", flip[0]) for send, flip in zip(sends, flips)]
    owns = [
        small_call(functools.partial(first_kernel, index), outs, keep, got)[0]
        for index, got in enumerate(gots)
    ]
    gots = [swap(own, "row", flip[1]) for own, flip in zip(owns, flips)]
    owns = [small_call(second_kernel, outs, own, got)[0] for own, got in zip(owns, gots)]
    gots = [swap(own, "row", flip[2]) for own, flip in zip(owns, flips)]
    result = None
    for index in range(2):
        result = place_half(index, bits, owns[index], gots[index], result)
    return result


def permute(value, pairs):
    return lax.ppermute(value, ("row", "col"), pairs)


def send_pieces(bits, panel, owners, after):
    lanes = panel.shape[1]
    rows = panel.shape[0] // LINE
    planes = [owner % PLANES for owner in owners]
    home_y, home_x = divmod(owners[0] // PLANES, LINE)

    def device(row, y, x, plane):
        return ((row * LINE + y) * LINE + x) * PLANES + plane

    got = [
        permute(
            panel[x * rows : (x + 1) * rows],
            [(device(r, home_y, home_x, p), device(r, home_y, x, p)) for r, p in enumerate(planes)],
        )
        for x in range(LINE)
        if x != home_x
    ]
    shape = jax.ShapeDtypeStruct((rows // LINE, lanes), panel.dtype)
    pieces = small_call(
        functools.partial(strip_kernel, home_x), [shape] * LINE, bits, panel, *got,
        scalars=1, after=after,
    )
    got = [
        permute(
            pieces[y],
            [
                (device(r, home_y, x, p), device(r, y, x, p))
                for r, p in enumerate(planes)
                for x in range(LINE)
            ],
        )
        for y in range(LINE)
        if y != home_y
    ]
    piece = small_call(sum_kernel, [shape], pieces[home_y], *got)[0]
    got = [
        permute(
            piece,
            [
                (device(r, y, x, p), device(r, y, x, (p + step) % PLANES))
                for r, p in enumerate(planes)
                for y in range(LINE)
                for x in range(LINE)
            ],
        )
        for step in range(1, PLANES)
    ]
    return [piece, *got]


def on_device(grm_tiles, tile_row, tile_col, panel):
    row_index = lax.axis_index("row")
    col_index = lax.axis_index("col")
    col_count = lax.axis_size("col")
    row_count = lax.axis_size("row")
    lanes = panel.shape[1]
    offset = CTD * col_count - RT_DEV * row_count
    base_row = row_index * RT_DEV
    base_col = col_index * CTD
    owners = [(offset + row * RT_DEV) // CTD for row in range(row_count)]

    local_row = tile_row - base_row
    local_col = jnp.maximum(tile_col - base_col, 0)
    kind = jnp.where(tile_col < 0, 0, jnp.where(tile_col == offset + tile_row, 2, 1))
    high = row_index // 2
    low = (row_index + high) % 2
    core = col_index % 2
    chip = col_index // 2 % 2
    root = (col_index == (offset + base_row) // CTD).astype(jnp.int32)
    bits = jnp.stack([low, high, core, chip, root]).astype(jnp.int32)
    info = jnp.stack(
        [local_row, local_col, kind, jnp.pad(bits[:2], (0, 2)), jnp.pad(bits[2:4], (0, 2))]
    ).astype(jnp.int32)

    across = [[site_at(place) * PLANES + plane for place in range(SITES)] for plane in range(PLANES)]
    tiles = pltpu.with_memory_space_constraint(grm_tiles, pltpu.HBM)
    keep, send = row_products(info, tiles, panel)
    half = keep.shape[0] // 2
    share = half // SITES
    mine, send_z = small_call(
        add_kernel, [floats(half, lanes), coded(half, lanes)], keep, swap(send, "col", 1)
    )
    pieces = send_pieces(bits, panel, owners, keep)
    size = pieces[0].shape[0]
    packed = small_call(
        pack_kernel,
        [jax.ShapeDtypeStruct((SITES, size + 2 * share, lanes), jnp.bfloat16)],
        mine, swap(send_z, "col", 2), *pieces,
    )[0]
    packed = lax.all_to_all(packed, "col", 0, 0, axis_index_groups=across)
    y_rows, keep, *sends = col_products(info, tiles, packed, share)
    y_cols = sum_over_row(bits, keep, sends)
    return (y_rows, y_cols)


def solution(mesh):
    in_specs = (P(("row", "col"), None, None), P(("row", "col")), P(("row", "col")), P("col", None))
    out_specs = (P(("row", "col"), None), P("col", None))
    return jax.shard_map(
        on_device, mesh=mesh, in_specs=in_specs, out_specs=out_specs, check_vma=False
    )
```

```python
import functools

import jax
import jax.numpy as jnp
from jax import lax
from jax.experimental import pallas as pl
from jax.experimental.pallas import tpu as pltpu
from jax.sharding import PartitionSpec as P

RT_DEV = 2
CTD = 2
STEPS = 2
MIB = 1024 * 1024
PAD = 16
SITES = 16
PLANES = 4
BF16_MOST = 3.3895313892515355e38


def place_of(info, index, depth, width):
    slot = index // STEPS
    part = index % STEPS
    local_row = info[0, slot]
    local_col = info[1, slot]
    first = pl.multiple_of(local_row * width + part * depth, depth)
    rows = pl.ds(first, depth)
    cols = pl.ds(pl.multiple_of(local_col * width, width), width)
    piece = pl.ds(pl.multiple_of(part * depth, depth), depth)
    return slot, part, rows, cols, piece


def fetch_of(info, tiles_ref, held, sems):
    slots, width, _ = held.shape
    depth = width // STEPS

    def fetch(index):
        slot, part, rows, cols, piece = place_of(info, index, depth, width)
        return pltpu.make_async_copy(
            tiles_ref.at[slot, piece], held.at[slot, piece], sems.at[index]
        )

    return fetch


def row_kernel(info, tiles_ref, panel_ref, keep_ref, send_ref, total, held, sems):
    slots, width, _ = held.shape
    depth = width // STEPS
    fetch = fetch_of(info, tiles_ref, held, sems)
    for index in range(slots * STEPS):
        fetch(index).start()
    total[...] = jnp.zeros_like(total)

    @pl.loop(0, slots * STEPS)
    def _(index):
        slot, part, rows, cols, piece = place_of(info, index, depth, width)
        kind = info[2, slot]
        fetch(index).wait()

        @pl.when(kind == 1)
        def _():
            total[rows, :] += jnp.dot(
                held[slot, piece, :], panel_ref[cols, :], preferred_element_type=jnp.float32
            )

        @pl.when(kind == 2)
        def _():
            row_ids = lax.broadcasted_iota(jnp.int32, (depth, width), 0) + part * depth
            col_ids = lax.broadcasted_iota(jnp.int32, (depth, width), 1)
            tile = held[slot, piece, :].astype(jnp.float32)
            lower = jnp.where(row_ids >= col_ids, tile, 0.0).astype(jnp.bfloat16)
            strict = jnp.where(row_ids > col_ids, tile, 0.0).astype(jnp.bfloat16)
            total[rows, :] += jnp.dot(lower, panel_ref[cols, :], preferred_element_type=jnp.float32)
            own = pl.ds(pl.multiple_of(info[1, slot] * width + part * depth, depth), depth)
            whole = pl.ds(pl.multiple_of(info[0, slot] * width, width), width)
            total[whole, :] += lax.dot_general(
                panel_ref[own, :], strict, (((0,), (0,)), ((), ())),
                preferred_element_type=jnp.float32,
            ).T

    core = info[4, 0]
    depth_z = info[4, 1]
    share = total.shape[0] // (SITES * PLANES)
    for ref, which in ((keep_ref, core), (send_ref, 1 - core)):
        for step, chip in enumerate((depth_z, 1 - depth_z)):
            for site in range(SITES):
                source = pl.multiple_of((site * PLANES + chip * 2 + which) * share, share)
                target = (step * SITES + site) * share
                ref[target : target + share, :] = total[pl.ds(source, share), :]


def add_kernel(keep_ref, got_ref, mine_ref, send_ref):
    size = mine_ref.shape[0]
    mine_ref[...] = keep_ref[:size, :] + got_ref[:size, :]
    encode(keep_ref[size:, :] + got_ref[size:, :], send_ref)


def pack_kernel(bits, piece_ref, got1_ref, got2_ref, got3_ref, out_ref):
    own = jnp.where(bits[4] == 1, piece_ref[...].astype(jnp.float32), 0.0)
    rest = got1_ref[...].astype(jnp.float32) + got2_ref[...].astype(jnp.float32)
    piece = (own + rest + got3_ref[...].astype(jnp.float32)).astype(jnp.bfloat16)
    for site in range(out_ref.shape[0]):
        out_ref[site] = piece


def rows_kernel(mine_ref, got_ref, after_ref, out_ref):
    del after_ref
    out_ref[...] = mine_ref[...] + decode(got_ref)


def total_kernel(terms_ref, out_ref):
    total = terms_ref[0]
    for site in range(1, terms_ref.shape[0]):
        total += terms_ref[site]
    out_ref[...] = total


def block_rows(size):
    return min(128, size)


def encode(value, out_ref):
    size = value.shape[0]
    block = block_rows(size)
    lanes = value.shape[1]
    powers = []
    for start in range(0, size, block):
        part = value[start : start + block]
        most = jnp.max(jnp.abs(part), axis=0, keepdims=True)
        power = 15.0 - jnp.maximum(jnp.ceil(jnp.log2(most)), -126.0)
        half = jnp.floor(power * 0.5)
        scaled = part * jnp.exp2(half) * jnp.exp2(power - half)
        whole = jnp.clip(jnp.round(scaled), -32767.0, 32767.0)
        out_ref[start : start + block, :] = whole.astype(jnp.int32).astype(jnp.int16)
        powers.append(power)
    powers.append(jnp.zeros((PAD - len(powers), lanes), jnp.float32))
    tail = jnp.concatenate(powers, axis=0)
    out_ref[size:, :] = tail.astype(jnp.int32).astype(jnp.int16)


def decode(ref):
    size = ref.shape[0] - PAD
    block = block_rows(size)
    tail = ref[size:, :].astype(jnp.int32).astype(jnp.float32)
    parts = []
    for index in range(size // block):
        power = tail[index : index + 1]
        half = jnp.floor(power * 0.5)
        part = ref[index * block : (index + 1) * block, :].astype(jnp.int32).astype(jnp.float32)
        parts.append(part * jnp.exp2(-half) * jnp.exp2(half - power))
    return jnp.concatenate(parts, axis=0)


def col_kernel(
    info, tiles_ref, slab_ref, after_ref, keep_ref, send0_ref, send1_ref, total, result, held, sems
):
    del after_ref
    slots, width, _ = held.shape
    depth = width // STEPS
    count = depth // slab_ref.shape[1]
    fetch = fetch_of(info, tiles_ref, held, sems)
    for index in range(slots * STEPS):
        fetch(index).start()
    total[...] = jnp.zeros_like(total)

    @pl.loop(0, slots * STEPS)
    def _(index):
        slot, part, rows, cols, piece = place_of(info, index, depth, width)
        fetch(index).wait()

        @pl.when(info[2, slot] == 1)
        def _():
            first = (info[0, slot] * STEPS + part) * count
            source = slab_ref[pl.ds(first, count), :, :].reshape(depth, slab_ref.shape[2])
            total[:, cols] += lax.dot_general(
                source, held[slot, piece, :], (((0,), (0,)), ((), ())),
                preferred_element_type=jnp.float32,
            )

    result[...] = total[...].T
    half = width // 2
    for index, send_ref in enumerate((send0_ref, send1_ref)):
        bit = info[3, index]
        mine = pl.multiple_of(index * width + bit * half, half)
        other = pl.multiple_of(index * width + (1 - bit) * half, half)
        keep_ref[index] = result[pl.ds(mine, half), :]
        encode(result[pl.ds(other, half), :], send_ref)


def first_kernel(index, keep_ref, got_ref, out_ref):
    encode(keep_ref[index] + decode(got_ref), out_ref)


def second_kernel(own_ref, got_ref, out_ref):
    encode(decode(own_ref) + decode(got_ref), out_ref)


def place_kernel(index, bits, own_ref, got_ref, *refs):
    out_ref, held, sem = refs[-3:]
    size = own_ref.shape[0] - PAD
    mine = pl.multiple_of(bits[index] * size, size)
    other = pl.multiple_of((1 - bits[index]) * size, size)
    held[pl.ds(mine, size), :] = decode(own_ref)
    held[pl.ds(other, size), :] = decode(got_ref)
    copy = pltpu.make_async_copy(held, out_ref.at[pl.ds(index * 2 * size, 2 * size)], sem)
    copy.start()
    copy.wait()


VMEM = pl.BlockSpec(memory_space=pltpu.VMEM)
SMEM = pl.BlockSpec(memory_space=pltpu.SMEM)
HBM = pl.BlockSpec(memory_space=pltpu.HBM)


def limit(size):
    return pltpu.CompilerParams(vmem_limit_bytes=size * MIB)


def small_call(kernel, outs, *args, scalars=0):
    return pl.pallas_call(
        kernel,
        in_specs=[SMEM] * scalars + [VMEM] * (len(args) - scalars),
        out_specs=[VMEM] * len(outs),
        out_shape=outs,
        compiler_params=limit(6),
    )(*args)


def place_half(index, bits, own, got, result):
    size, lanes = own.shape[0] - PAD, own.shape[1]
    args = (bits, own, got) + (() if result is None else (result,))
    return pl.pallas_call(
        functools.partial(place_kernel, index),
        in_specs=[SMEM, VMEM, VMEM] + [HBM] * (len(args) - 3),
        out_specs=HBM,
        out_shape=floats(4 * size, lanes),
        scratch_shapes=[pltpu.VMEM((2 * size, lanes), jnp.float32), pltpu.SemaphoreType.DMA],
        input_output_aliases={} if result is None else {3: 0},
        compiler_params=limit(6),
    )(*args)


def tile_cost(shape, lanes):
    slots, width, _ = shape
    return pl.CostEstimate(
        flops=2 * slots * width * width * lanes,
        bytes_accessed=2 * slots * width * width + 2 * MIB,
        transcendentals=0,
    )


def floats(*shape):
    return jax.ShapeDtypeStruct(shape, jnp.float32)


def coded(size, lanes):
    return jax.ShapeDtypeStruct((size + PAD, lanes), jnp.int16)


def tile_scratch(grm_tiles):
    return [
        pltpu.VMEM(grm_tiles.shape, grm_tiles.dtype),
        pltpu.SemaphoreType.DMA((grm_tiles.shape[0] * STEPS,)),
    ]


def row_products(info, grm_tiles, panel):
    slots, width, _ = grm_tiles.shape
    lanes = panel.shape[1]
    rows = RT_DEV * width
    return pl.pallas_call(
        row_kernel,
        in_specs=[SMEM, HBM, VMEM],
        out_specs=[VMEM, VMEM],
        out_shape=[floats(rows // 2, lanes), floats(rows // 2, lanes)],
        scratch_shapes=[pltpu.VMEM((rows, lanes), jnp.float32)] + tile_scratch(grm_tiles),
        compiler_params=limit(24),
        cost_estimate=tile_cost(grm_tiles.shape, lanes),
    )(info, grm_tiles, panel)


def col_products(info, grm_tiles, slab, after):
    slots, width, _ = grm_tiles.shape
    lanes = slab.shape[2]
    half = width // 2
    return pl.pallas_call(
        col_kernel,
        in_specs=[SMEM, HBM, VMEM, VMEM],
        out_specs=[VMEM] * 3,
        out_shape=[floats(2, half, lanes), coded(half, lanes), coded(half, lanes)],
        scratch_shapes=[
            pltpu.VMEM((lanes, CTD * width), jnp.float32),
            pltpu.VMEM((CTD * width, lanes), jnp.float32),
        ]
        + tile_scratch(grm_tiles),
        compiler_params=limit(24),
        cost_estimate=tile_cost(grm_tiles.shape, lanes),
    )(info, grm_tiles, slab, after)


def swap(value, axis, flip):
    return lax.ppermute(value, axis, [(k, k ^ flip) for k in range(lax.axis_size(axis))])


def sum_over_row(bits, keep, sends):
    size, lanes = keep.shape[1:]
    outs = [coded(size, lanes)]
    flips = [(1, 3, 1), (3, 1, 3)]
    gots = [swap(send, "row", flip[0]) for send, flip in zip(sends, flips)]
    owns = [
        small_call(functools.partial(first_kernel, index), outs, keep, got)[0]
        for index, got in enumerate(gots)
    ]
    begun = owns[0]
    gots = [swap(own, "row", flip[1]) for own, flip in zip(owns, flips)]
    owns = [small_call(second_kernel, outs, own, got)[0] for own, got in zip(owns, gots)]
    gots = [swap(own, "row", flip[2]) for own, flip in zip(owns, flips)]
    result = None
    for index in range(2):
        result = place_half(index, bits, owns[index], gots[index], result)
    return result, begun


def spread(piece, planes):
    got = []
    for step in range(1, PLANES):
        pairs = [
            ((row * SITES + site) * PLANES + plane, (row * SITES + site) * PLANES + (plane + step) % PLANES)
            for row, plane in enumerate(planes)
            for site in range(SITES)
        ]
        got.append(lax.ppermute(piece, ("row", "col"), pairs))
    return got


def on_device(grm_tiles, tile_row, tile_col, panel):
    row_index = lax.axis_index("row")
    col_index = lax.axis_index("col")
    col_count = lax.axis_size("col")
    row_count = lax.axis_size("row")
    lanes = panel.shape[1]
    offset = CTD * col_count - RT_DEV * row_count
    base_row = row_index * RT_DEV
    base_col = col_index * CTD
    owners = [(offset + row * RT_DEV) // CTD for row in range(row_count)]

    local_row = tile_row - base_row
    local_col = jnp.maximum(tile_col - base_col, 0)
    kind = jnp.where(tile_col < 0, 0, jnp.where(tile_col == offset + tile_row, 2, 1))
    high = row_index // 2
    low = (row_index + high) % 2
    core = col_index % 2
    chip = col_index // 2 % 2
    holds = (col_index % PLANES == (offset + base_row) // CTD % PLANES).astype(jnp.int32)
    bits = jnp.stack([low, high, core, chip, holds]).astype(jnp.int32)
    info = jnp.stack(
        [local_row, local_col, kind, jnp.pad(bits[:2], (0, 2)), jnp.pad(bits[2:4], (0, 2))]
    ).astype(jnp.int32)

    across = [[site * PLANES + plane for site in range(SITES)] for plane in range(PLANES)]
    tiles = pltpu.with_memory_space_constraint(grm_tiles, pltpu.HBM)
    size = panel.shape[0] // SITES
    pieces = lax.all_to_all(
        panel.reshape(SITES, size, lanes), "col", 0, 0, axis_index_groups=across
    )
    keep, send = row_products(info, tiles, panel)
    pieces, keep, send = lax.optimization_barrier((pieces, keep, send))
    half = keep.shape[0] // 2
    share = half // SITES
    mine, send_z = small_call(
        add_kernel, [floats(half, lanes), coded(half, lanes)], keep, swap(send, "col", 1)
    )
    piece = pieces[owners[0] // PLANES]
    got = spread(piece, [owner % PLANES for owner in owners])
    packed = small_call(
        pack_kernel,
        [jax.ShapeDtypeStruct((SITES, size, lanes), jnp.bfloat16)],
        bits, piece, *got,
        scalars=1,
    )[0]
    slab = lax.all_to_all(packed, "col", 0, 0, axis_index_groups=across)
    got_z = swap(send_z, "col", 2)
    keep, *sends = col_products(info, tiles, slab, got_z)
    y_cols, begun = sum_over_row(bits, keep, sends)
    rows = small_call(rows_kernel, [floats(half, lanes)], mine, got_z, begun)[0]
    terms = lax.all_to_all(
        rows.reshape(SITES, share, lanes), "col", 0, 0, axis_index_groups=across
    )
    y_rows = small_call(total_kernel, [floats(share, lanes)], terms)[0]
    return (y_rows, y_cols)


def solution(mesh):
    in_specs = (P(("row", "col"), None, None), P(("row", "col")), P(("row", "col")), P("col", None))
    out_specs = (P(("row", "col"), None), P("col", None))
    return jax.shard_map(
        on_device, mesh=mesh, in_specs=in_specs, out_specs=out_specs, check_vma=False
    )
```

```python
import functools

import jax
import jax.numpy as jnp
from jax import lax
from jax.experimental import pallas as pl
from jax.experimental.pallas import tpu as pltpu
from jax.sharding import PartitionSpec as P

RT_DEV = 2
CTD = 2
STEPS = 2
MIB = 1024 * 1024
PAD = 16
SITES = 16
PLANES = 4
BF16_MOST = 3.3895313892515355e38


def place_of(info, index, depth, width):
    slot = index // STEPS
    part = index % STEPS
    local_row = info[0, slot]
    local_col = info[1, slot]
    first = pl.multiple_of(local_row * width + part * depth, depth)
    rows = pl.ds(first, depth)
    cols = pl.ds(pl.multiple_of(local_col * width, width), width)
    piece = pl.ds(pl.multiple_of(part * depth, depth), depth)
    return slot, part, rows, cols, piece


def fetch_of(info, tiles_ref, held, sems):
    slots, width, _ = held.shape
    depth = width // STEPS

    def fetch(index):
        slot, part, rows, cols, piece = place_of(info, index, depth, width)
        return pltpu.make_async_copy(
            tiles_ref.at[slot, piece], held.at[slot, piece], sems.at[index]
        )

    return fetch


def row_kernel(info, tiles_ref, panel_ref, keep_ref, send_ref, total, held, sems):
    slots, width, _ = held.shape
    depth = width // STEPS
    fetch = fetch_of(info, tiles_ref, held, sems)
    for index in range(slots * STEPS):
        fetch(index).start()
    total[...] = jnp.zeros_like(total)

    @pl.loop(0, slots * STEPS)
    def _(index):
        slot, part, rows, cols, piece = place_of(info, index, depth, width)
        kind = info[2, slot]
        fetch(index).wait()

        @pl.when(kind == 1)
        def _():
            total[rows, :] += jnp.dot(
                held[slot, piece, :], panel_ref[cols, :], preferred_element_type=jnp.float32
            )

        @pl.when(kind == 2)
        def _():
            row_ids = lax.broadcasted_iota(jnp.int32, (depth, width), 0) + part * depth
            col_ids = lax.broadcasted_iota(jnp.int32, (depth, width), 1)
            tile = held[slot, piece, :].astype(jnp.float32)
            lower = jnp.where(row_ids >= col_ids, tile, 0.0).astype(jnp.bfloat16)
            strict = jnp.where(row_ids > col_ids, tile, 0.0).astype(jnp.bfloat16)
            total[rows, :] += jnp.dot(lower, panel_ref[cols, :], preferred_element_type=jnp.float32)
            own = pl.ds(pl.multiple_of(info[1, slot] * width + part * depth, depth), depth)
            whole = pl.ds(pl.multiple_of(info[0, slot] * width, width), width)
            total[whole, :] += lax.dot_general(
                panel_ref[own, :], strict, (((0,), (0,)), ((), ())),
                preferred_element_type=jnp.float32,
            ).T

    core = info[4, 0]
    depth_z = info[4, 1]
    share = total.shape[0] // (SITES * PLANES)
    for ref, which in ((keep_ref, core), (send_ref, 1 - core)):
        for step, chip in enumerate((depth_z, 1 - depth_z)):
            for site in range(SITES):
                source = pl.multiple_of((site * PLANES + chip * 2 + which) * share, share)
                target = (step * SITES + site) * share
                ref[target : target + share, :] = total[pl.ds(source, share), :]


def add_kernel(keep_ref, got_ref, mine_ref, send_ref):
    size = mine_ref.shape[0]
    mine_ref[...] = keep_ref[:size, :] + got_ref[:size, :]
    encode(keep_ref[size:, :] + got_ref[size:, :], send_ref)


def select_kernel(bits, own_ref, got_ref, out_ref):
    @pl.when(bits[4] == 1)
    def _():
        out_ref[...] = own_ref[...]

    @pl.when(bits[4] == 0)
    def _():
        out_ref[...] = got_ref[...]


def pack_kernel(bits, mine_ref, got_ref, piece_ref, other_ref, out_ref):
    sites = out_ref.shape[0]
    size = piece_ref.shape[0]
    share = mine_ref.shape[0] // sites
    own = piece_ref[...].astype(jnp.float32)
    piece = jnp.where(bits[5] == 1, own, other_ref[...].astype(jnp.float32)).astype(jnp.bfloat16)
    sums = mine_ref[...] + decode(got_ref)
    high = jnp.clip(sums, -BF16_MOST, BF16_MOST).astype(jnp.bfloat16)
    low = (sums - high.astype(jnp.float32)).astype(jnp.bfloat16)
    for site in range(sites):
        out_ref[site, :size, :] = piece
        out_ref[site, size : size + share, :] = high[site * share : (site + 1) * share]
        out_ref[site, size + share :, :] = low[site * share : (site + 1) * share]


def block_rows(size):
    return min(128, size)


def encode(value, out_ref):
    size = value.shape[0]
    block = block_rows(size)
    lanes = value.shape[1]
    powers = []
    for start in range(0, size, block):
        part = value[start : start + block]
        most = jnp.max(jnp.abs(part), axis=0, keepdims=True)
        power = 15.0 - jnp.maximum(jnp.ceil(jnp.log2(most)), -126.0)
        half = jnp.floor(power * 0.5)
        scaled = part * jnp.exp2(half) * jnp.exp2(power - half)
        whole = jnp.clip(jnp.round(scaled), -32767.0, 32767.0)
        out_ref[start : start + block, :] = whole.astype(jnp.int32).astype(jnp.int16)
        powers.append(power)
    powers.append(jnp.zeros((PAD - len(powers), lanes), jnp.float32))
    tail = jnp.concatenate(powers, axis=0)
    out_ref[size:, :] = tail.astype(jnp.int32).astype(jnp.int16)


def decode(ref):
    size = ref.shape[0] - PAD
    block = block_rows(size)
    tail = ref[size:, :].astype(jnp.int32).astype(jnp.float32)
    parts = []
    for index in range(size // block):
        power = tail[index : index + 1]
        half = jnp.floor(power * 0.5)
        part = ref[index * block : (index + 1) * block, :].astype(jnp.int32).astype(jnp.float32)
        parts.append(part * jnp.exp2(-half) * jnp.exp2(half - power))
    return jnp.concatenate(parts, axis=0)


def col_kernel(
    info, tiles_ref, slab_ref, rows_ref, keep_ref, send0_ref, send1_ref, total, result, held, sems
):
    slots, width, _ = held.shape
    depth = width // STEPS
    size, share = slab_ref.shape[1], rows_ref.shape[0]
    size = size - 2 * share
    count = depth // size
    fetch = fetch_of(info, tiles_ref, held, sems)
    for index in range(slots * STEPS):
        fetch(index).start()
    total[...] = jnp.zeros_like(total)
    sums = jnp.zeros(rows_ref.shape, jnp.float32)
    for site in range(slab_ref.shape[0]):
        sums += slab_ref[site, size : size + share, :].astype(jnp.float32)
        sums += slab_ref[site, size + share :, :].astype(jnp.float32)
    rows_ref[...] = sums

    @pl.loop(0, slots * STEPS)
    def _(index):
        slot, part, rows, cols, piece = place_of(info, index, depth, width)
        fetch(index).wait()

        @pl.when(info[2, slot] == 1)
        def _():
            first = (info[0, slot] * STEPS + part) * count
            source = slab_ref[pl.ds(first, count), :size, :].reshape(depth, slab_ref.shape[2])
            total[:, cols] += lax.dot_general(
                source, held[slot, piece, :], (((0,), (0,)), ((), ())),
                preferred_element_type=jnp.float32,
            )

    result[...] = total[...].T
    half = width // 2
    for index, send_ref in enumerate((send0_ref, send1_ref)):
        bit = info[3, index]
        mine = pl.multiple_of(index * width + bit * half, half)
        other = pl.multiple_of(index * width + (1 - bit) * half, half)
        keep_ref[index] = result[pl.ds(mine, half), :]
        encode(result[pl.ds(other, half), :], send_ref)


def first_kernel(index, keep_ref, got_ref, out_ref):
    encode(keep_ref[index] + decode(got_ref), out_ref)


def second_kernel(own_ref, got_ref, out_ref):
    encode(decode(own_ref) + decode(got_ref), out_ref)


def place_kernel(index, bits, own_ref, got_ref, *refs):
    out_ref, held, sem = refs[-3:]
    size = own_ref.shape[0] - PAD
    mine = pl.multiple_of(bits[index] * size, size)
    other = pl.multiple_of((1 - bits[index]) * size, size)
    held[pl.ds(mine, size), :] = decode(own_ref)
    held[pl.ds(other, size), :] = decode(got_ref)
    copy = pltpu.make_async_copy(held, out_ref.at[pl.ds(index * 2 * size, 2 * size)], sem)
    copy.start()
    copy.wait()


VMEM = pl.BlockSpec(memory_space=pltpu.VMEM)
SMEM = pl.BlockSpec(memory_space=pltpu.SMEM)
HBM = pl.BlockSpec(memory_space=pltpu.HBM)


def limit(size):
    return pltpu.CompilerParams(vmem_limit_bytes=size * MIB)


def small_call(kernel, outs, *args, scalars=0):
    return pl.pallas_call(
        kernel,
        in_specs=[SMEM] * scalars + [VMEM] * (len(args) - scalars),
        out_specs=[VMEM] * len(outs),
        out_shape=outs,
        compiler_params=limit(6),
    )(*args)


def place_half(index, bits, own, got, result):
    size, lanes = own.shape[0] - PAD, own.shape[1]
    args = (bits, own, got) + (() if result is None else (result,))
    return pl.pallas_call(
        functools.partial(place_kernel, index),
        in_specs=[SMEM, VMEM, VMEM] + [HBM] * (len(args) - 3),
        out_specs=HBM,
        out_shape=floats(4 * size, lanes),
        scratch_shapes=[pltpu.VMEM((2 * size, lanes), jnp.float32), pltpu.SemaphoreType.DMA],
        input_output_aliases={} if result is None else {3: 0},
        compiler_params=limit(6),
    )(*args)


def tile_cost(shape, lanes):
    slots, width, _ = shape
    return pl.CostEstimate(
        flops=2 * slots * width * width * lanes,
        bytes_accessed=2 * slots * width * width + 2 * MIB,
        transcendentals=0,
    )


def floats(*shape):
    return jax.ShapeDtypeStruct(shape, jnp.float32)


def coded(size, lanes):
    return jax.ShapeDtypeStruct((size + PAD, lanes), jnp.int16)


def tile_scratch(grm_tiles):
    return [
        pltpu.VMEM(grm_tiles.shape, grm_tiles.dtype),
        pltpu.SemaphoreType.DMA((grm_tiles.shape[0] * STEPS,)),
    ]


def row_products(info, grm_tiles, panel):
    slots, width, _ = grm_tiles.shape
    lanes = panel.shape[1]
    rows = RT_DEV * width
    return pl.pallas_call(
        row_kernel,
        in_specs=[SMEM, HBM, VMEM],
        out_specs=[VMEM, VMEM],
        out_shape=[floats(rows // 2, lanes), floats(rows // 2, lanes)],
        scratch_shapes=[pltpu.VMEM((rows, lanes), jnp.float32)] + tile_scratch(grm_tiles),
        compiler_params=limit(24),
        cost_estimate=tile_cost(grm_tiles.shape, lanes),
    )(info, grm_tiles, panel)


def col_products(info, grm_tiles, packed, share):
    slots, width, _ = grm_tiles.shape
    lanes = packed.shape[2]
    half = width // 2
    return pl.pallas_call(
        col_kernel,
        in_specs=[SMEM, HBM, VMEM],
        out_specs=[VMEM] * 4,
        out_shape=[floats(share, lanes), floats(2, half, lanes), coded(half, lanes), coded(half, lanes)],
        scratch_shapes=[
            pltpu.VMEM((lanes, CTD * width), jnp.float32),
            pltpu.VMEM((CTD * width, lanes), jnp.float32),
        ]
        + tile_scratch(grm_tiles),
        compiler_params=limit(24),
        cost_estimate=tile_cost(grm_tiles.shape, lanes),
    )(info, grm_tiles, packed)


def swap(value, axis, flip):
    return lax.ppermute(value, axis, [(k, k ^ flip) for k in range(lax.axis_size(axis))])


def sum_over_row(bits, keep, sends):
    size, lanes = keep.shape[1:]
    outs = [coded(size, lanes)]
    flips = [(1, 3, 1), (3, 1, 3)]
    gots = [swap(send, "row", flip[0]) for send, flip in zip(sends, flips)]
    owns = [
        small_call(functools.partial(first_kernel, index), outs, keep, got)[0]
        for index, got in enumerate(gots)
    ]
    gots = [swap(own, "row", flip[1]) for own, flip in zip(owns, flips)]
    owns = [small_call(second_kernel, outs, own, got)[0] for own, got in zip(owns, gots)]
    gots = [swap(own, "row", flip[2]) for own, flip in zip(owns, flips)]
    result = None
    for index in range(2):
        result = place_half(index, bits, owns[index], gots[index], result)
    return result


def on_device(grm_tiles, tile_row, tile_col, panel):
    row_index = lax.axis_index("row")
    col_index = lax.axis_index("col")
    col_count = lax.axis_size("col")
    row_count = lax.axis_size("row")
    lanes = panel.shape[1]
    offset = CTD * col_count - RT_DEV * row_count
    base_row = row_index * RT_DEV
    base_col = col_index * CTD
    owners = [(offset + row * RT_DEV) // CTD for row in range(row_count)]

    local_row = tile_row - base_row
    local_col = jnp.maximum(tile_col - base_col, 0)
    kind = jnp.where(tile_col < 0, 0, jnp.where(tile_col == offset + tile_row, 2, 1))
    high = row_index // 2
    low = (row_index + high) % 2
    core = col_index % 2
    chip = col_index // 2 % 2
    root = (offset + base_row) // CTD
    bits = jnp.stack([low, high, core, chip, core == root % 2, chip == root // 2 % 2]).astype(jnp.int32)
    info = jnp.stack(
        [local_row, local_col, kind, jnp.pad(bits[:2], (0, 2)), jnp.pad(bits[2:4], (0, 2))]
    ).astype(jnp.int32)

    across = [[site * PLANES + plane for site in range(SITES)] for plane in range(PLANES)]
    tiles = pltpu.with_memory_space_constraint(grm_tiles, pltpu.HBM)
    size = panel.shape[0] // SITES
    pieces = lax.all_to_all(
        panel.reshape(SITES, size, lanes), "col", 0, 0, axis_index_groups=across
    )
    keep, send = row_products(info, tiles, panel)
    pieces, keep = lax.optimization_barrier((pieces, keep))
    half = keep.shape[0] // 2
    share = half // SITES
    mine, send_z = small_call(
        add_kernel, [floats(half, lanes), coded(half, lanes)], keep, swap(send, "col", 1)
    )
    piece = pieces[owners[0] // PLANES]
    outs = [jax.ShapeDtypeStruct((size, lanes), panel.dtype)]
    piece = small_call(select_kernel, outs, bits, piece, swap(piece, "col", 1), scalars=1)[0]
    packed = small_call(
        pack_kernel,
        [jax.ShapeDtypeStruct((SITES, size + 2 * share, lanes), jnp.bfloat16)],
        bits, mine, swap(send_z, "col", 2), piece, swap(piece, "col", 2),
        scalars=1,
    )[0]
    packed = lax.all_to_all(packed, "col", 0, 0, axis_index_groups=across)
    y_rows, keep, *sends = col_products(info, tiles, packed, share)
    y_cols = sum_over_row(bits, keep, sends)
    return (y_rows, y_cols)


def solution(mesh):
    in_specs = (P(("row", "col"), None, None), P(("row", "col")), P(("row", "col")), P("col", None))
    out_specs = (P(("row", "col"), None), P("col", None))
    return jax.shard_map(
        on_device, mesh=mesh, in_specs=in_specs, out_specs=out_specs, check_vma=False
    )
```

```python
import functools

import jax
import jax.numpy as jnp
from jax import lax
from jax.experimental import pallas as pl
from jax.experimental.pallas import tpu as pltpu
from jax.sharding import PartitionSpec as P

RT_DEV = 2
CTD = 2
STEPS = 2
MIB = 1024 * 1024
PAD = 16
SITES = 16
PLANES = 4
BF16_MOST = 3.3895313892515355e38


def place_of(info, index, depth, width):
    slot = index // STEPS
    part = index % STEPS
    local_row = info[0, slot]
    local_col = info[1, slot]
    first = pl.multiple_of(local_row * width + part * depth, depth)
    rows = pl.ds(first, depth)
    cols = pl.ds(pl.multiple_of(local_col * width, width), width)
    piece = pl.ds(pl.multiple_of(part * depth, depth), depth)
    return slot, part, rows, cols, piece


def fetch_of(info, tiles_ref, held, sems):
    slots, width, _ = held.shape
    depth = width // STEPS

    def fetch(index):
        slot, part, rows, cols, piece = place_of(info, index, depth, width)
        return pltpu.make_async_copy(
            tiles_ref.at[slot, piece], held.at[slot, piece], sems.at[index]
        )

    return fetch


def row_kernel(info, tiles_ref, panel_ref, keep_ref, send_ref, total, held, sems):
    slots, width, _ = held.shape
    depth = width // STEPS
    fetch = fetch_of(info, tiles_ref, held, sems)
    for index in range(slots * STEPS):
        fetch(index).start()
    total[...] = jnp.zeros_like(total)

    @pl.loop(0, slots * STEPS)
    def _(index):
        slot, part, rows, cols, piece = place_of(info, index, depth, width)
        kind = info[2, slot]
        fetch(index).wait()

        @pl.when(kind == 1)
        def _():
            total[rows, :] += jnp.dot(
                held[slot, piece, :], panel_ref[cols, :], preferred_element_type=jnp.float32
            )

        @pl.when(kind == 2)
        def _():
            row_ids = lax.broadcasted_iota(jnp.int32, (depth, width), 0) + part * depth
            col_ids = lax.broadcasted_iota(jnp.int32, (depth, width), 1)
            tile = held[slot, piece, :].astype(jnp.float32)
            lower = jnp.where(row_ids >= col_ids, tile, 0.0).astype(jnp.bfloat16)
            strict = jnp.where(row_ids > col_ids, tile, 0.0).astype(jnp.bfloat16)
            total[rows, :] += jnp.dot(lower, panel_ref[cols, :], preferred_element_type=jnp.float32)
            own = pl.ds(pl.multiple_of(info[1, slot] * width + part * depth, depth), depth)
            whole = pl.ds(pl.multiple_of(info[0, slot] * width, width), width)
            total[whole, :] += lax.dot_general(
                panel_ref[own, :], strict, (((0,), (0,)), ((), ())),
                preferred_element_type=jnp.float32,
            ).T

    core = info[4, 0]
    depth_z = info[4, 1]
    share = total.shape[0] // (SITES * PLANES)
    for ref, which in ((keep_ref, core), (send_ref, 1 - core)):
        for step, chip in enumerate((depth_z, 1 - depth_z)):
            for site in range(SITES):
                source = pl.multiple_of((site * PLANES + chip * 2 + which) * share, share)
                target = (step * SITES + site) * share
                ref[target : target + share, :] = total[pl.ds(source, share), :]


def add_kernel(keep_ref, got_ref, mine_ref, send_ref):
    size = mine_ref.shape[0]
    mine_ref[...] = keep_ref[:size, :] + got_ref[:size, :]
    encode(keep_ref[size:, :] + got_ref[size:, :], send_ref)


def select_kernel(bits, own_ref, got_ref, out_ref):
    @pl.when(bits[4] == 1)
    def _():
        out_ref[...] = own_ref[...]

    @pl.when(bits[4] == 0)
    def _():
        out_ref[...] = got_ref[...]


def pack_kernel(bits, piece_ref, other_ref, out_ref):
    own = piece_ref[...].astype(jnp.float32)
    piece = jnp.where(bits[5] == 1, own, other_ref[...].astype(jnp.float32)).astype(jnp.bfloat16)
    for site in range(out_ref.shape[0]):
        out_ref[site] = piece


def rows_kernel(mine_ref, got_ref, after_ref, out_ref):
    del after_ref
    out_ref[...] = mine_ref[...] + decode(got_ref)


def total_kernel(terms_ref, out_ref):
    total = terms_ref[0]
    for site in range(1, terms_ref.shape[0]):
        total += terms_ref[site]
    out_ref[...] = total


def block_rows(size):
    return min(128, size)


def encode(value, out_ref):
    size = value.shape[0]
    block = block_rows(size)
    lanes = value.shape[1]
    powers = []
    for start in range(0, size, block):
        part = value[start : start + block]
        most = jnp.max(jnp.abs(part), axis=0, keepdims=True)
        power = 15.0 - jnp.maximum(jnp.ceil(jnp.log2(most)), -126.0)
        half = jnp.floor(power * 0.5)
        scaled = part * jnp.exp2(half) * jnp.exp2(power - half)
        whole = jnp.clip(jnp.round(scaled), -32767.0, 32767.0)
        out_ref[start : start + block, :] = whole.astype(jnp.int32).astype(jnp.int16)
        powers.append(power)
    powers.append(jnp.zeros((PAD - len(powers), lanes), jnp.float32))
    tail = jnp.concatenate(powers, axis=0)
    out_ref[size:, :] = tail.astype(jnp.int32).astype(jnp.int16)


def decode(ref):
    size = ref.shape[0] - PAD
    block = block_rows(size)
    tail = ref[size:, :].astype(jnp.int32).astype(jnp.float32)
    parts = []
    for index in range(size // block):
        power = tail[index : index + 1]
        half = jnp.floor(power * 0.5)
        part = ref[index * block : (index + 1) * block, :].astype(jnp.int32).astype(jnp.float32)
        parts.append(part * jnp.exp2(-half) * jnp.exp2(half - power))
    return jnp.concatenate(parts, axis=0)


def col_kernel(
    info, tiles_ref, slab_ref, after_ref, keep_ref, send0_ref, send1_ref, total, result, held, sems
):
    del after_ref
    slots, width, _ = held.shape
    depth = width // STEPS
    count = depth // slab_ref.shape[1]
    fetch = fetch_of(info, tiles_ref, held, sems)
    for index in range(slots * STEPS):
        fetch(index).start()
    total[...] = jnp.zeros_like(total)

    @pl.loop(0, slots * STEPS)
    def _(index):
        slot, part, rows, cols, piece = place_of(info, index, depth, width)
        fetch(index).wait()

        @pl.when(info[2, slot] == 1)
        def _():
            first = (info[0, slot] * STEPS + part) * count
            source = slab_ref[pl.ds(first, count), :, :].reshape(depth, slab_ref.shape[2])
            total[:, cols] += lax.dot_general(
                source, held[slot, piece, :], (((0,), (0,)), ((), ())),
                preferred_element_type=jnp.float32,
            )

    result[...] = total[...].T
    half = width // 2
    for index, send_ref in enumerate((send0_ref, send1_ref)):
        bit = info[3, index]
        mine = pl.multiple_of(index * width + bit * half, half)
        other = pl.multiple_of(index * width + (1 - bit) * half, half)
        keep_ref[index] = result[pl.ds(mine, half), :]
        encode(result[pl.ds(other, half), :], send_ref)


def first_kernel(index, keep_ref, got_ref, out_ref):
    encode(keep_ref[index] + decode(got_ref), out_ref)


def second_kernel(own_ref, got_ref, out_ref):
    encode(decode(own_ref) + decode(got_ref), out_ref)


def place_kernel(index, bits, own_ref, got_ref, *refs):
    out_ref, held, sem = refs[-3:]
    size = own_ref.shape[0] - PAD
    mine = pl.multiple_of(bits[index] * size, size)
    other = pl.multiple_of((1 - bits[index]) * size, size)
    held[pl.ds(mine, size), :] = decode(own_ref)
    held[pl.ds(other, size), :] = decode(got_ref)
    copy = pltpu.make_async_copy(held, out_ref.at[pl.ds(index * 2 * size, 2 * size)], sem)
    copy.start()
    copy.wait()


VMEM = pl.BlockSpec(memory_space=pltpu.VMEM)
SMEM = pl.BlockSpec(memory_space=pltpu.SMEM)
HBM = pl.BlockSpec(memory_space=pltpu.HBM)


def limit(size):
    return pltpu.CompilerParams(vmem_limit_bytes=size * MIB)


def small_call(kernel, outs, *args, scalars=0):
    return pl.pallas_call(
        kernel,
        in_specs=[SMEM] * scalars + [VMEM] * (len(args) - scalars),
        out_specs=[VMEM] * len(outs),
        out_shape=outs,
        compiler_params=limit(6),
    )(*args)


def place_half(index, bits, own, got, result):
    size, lanes = own.shape[0] - PAD, own.shape[1]
    args = (bits, own, got) + (() if result is None else (result,))
    return pl.pallas_call(
        functools.partial(place_kernel, index),
        in_specs=[SMEM, VMEM, VMEM] + [HBM] * (len(args) - 3),
        out_specs=HBM,
        out_shape=floats(4 * size, lanes),
        scratch_shapes=[pltpu.VMEM((2 * size, lanes), jnp.float32), pltpu.SemaphoreType.DMA],
        input_output_aliases={} if result is None else {3: 0},
        compiler_params=limit(6),
    )(*args)


def tile_cost(shape, lanes):
    slots, width, _ = shape
    return pl.CostEstimate(
        flops=2 * slots * width * width * lanes,
        bytes_accessed=2 * slots * width * width + 2 * MIB,
        transcendentals=0,
    )


def floats(*shape):
    return jax.ShapeDtypeStruct(shape, jnp.float32)


def coded(size, lanes):
    return jax.ShapeDtypeStruct((size + PAD, lanes), jnp.int16)


def tile_scratch(grm_tiles):
    return [
        pltpu.VMEM(grm_tiles.shape, grm_tiles.dtype),
        pltpu.SemaphoreType.DMA((grm_tiles.shape[0] * STEPS,)),
    ]


def row_products(info, grm_tiles, panel):
    slots, width, _ = grm_tiles.shape
    lanes = panel.shape[1]
    rows = RT_DEV * width
    return pl.pallas_call(
        row_kernel,
        in_specs=[SMEM, HBM, VMEM],
        out_specs=[VMEM, VMEM],
        out_shape=[floats(rows // 2, lanes), floats(rows // 2, lanes)],
        scratch_shapes=[pltpu.VMEM((rows, lanes), jnp.float32)] + tile_scratch(grm_tiles),
        compiler_params=limit(24),
        cost_estimate=tile_cost(grm_tiles.shape, lanes),
    )(info, grm_tiles, panel)


def col_products(info, grm_tiles, slab, after):
    slots, width, _ = grm_tiles.shape
    lanes = slab.shape[2]
    half = width // 2
    return pl.pallas_call(
        col_kernel,
        in_specs=[SMEM, HBM, VMEM, VMEM],
        out_specs=[VMEM] * 3,
        out_shape=[floats(2, half, lanes), coded(half, lanes), coded(half, lanes)],
        scratch_shapes=[
            pltpu.VMEM((lanes, CTD * width), jnp.float32),
            pltpu.VMEM((CTD * width, lanes), jnp.float32),
        ]
        + tile_scratch(grm_tiles),
        compiler_params=limit(24),
        cost_estimate=tile_cost(grm_tiles.shape, lanes),
    )(info, grm_tiles, slab, after)


def swap(value, axis, flip):
    return lax.ppermute(value, axis, [(k, k ^ flip) for k in range(lax.axis_size(axis))])


def sum_over_row(bits, keep, sends):
    size, lanes = keep.shape[1:]
    outs = [coded(size, lanes)]
    flips = [(1, 3, 1), (3, 1, 3)]
    gots = [swap(send, "row", flip[0]) for send, flip in zip(sends, flips)]
    owns = [
        small_call(functools.partial(first_kernel, index), outs, keep, got)[0]
        for index, got in enumerate(gots)
    ]
    begun = owns[0]
    gots = [swap(own, "row", flip[1]) for own, flip in zip(owns, flips)]
    owns = [small_call(second_kernel, outs, own, got)[0] for own, got in zip(owns, gots)]
    gots = [swap(own, "row", flip[2]) for own, flip in zip(owns, flips)]
    result = None
    for index in range(2):
        result = place_half(index, bits, owns[index], gots[index], result)
    return result, begun


def on_device(grm_tiles, tile_row, tile_col, panel):
    row_index = lax.axis_index("row")
    col_index = lax.axis_index("col")
    col_count = lax.axis_size("col")
    row_count = lax.axis_size("row")
    lanes = panel.shape[1]
    offset = CTD * col_count - RT_DEV * row_count
    base_row = row_index * RT_DEV
    base_col = col_index * CTD
    owners = [(offset + row * RT_DEV) // CTD for row in range(row_count)]

    local_row = tile_row - base_row
    local_col = jnp.maximum(tile_col - base_col, 0)
    kind = jnp.where(tile_col < 0, 0, jnp.where(tile_col == offset + tile_row, 2, 1))
    high = row_index // 2
    low = (row_index + high) % 2
    core = col_index % 2
    chip = col_index // 2 % 2
    root = (offset + base_row) // CTD
    bits = jnp.stack([low, high, core, chip, core == root % 2, chip == root // 2 % 2]).astype(jnp.int32)
    info = jnp.stack(
        [local_row, local_col, kind, jnp.pad(bits[:2], (0, 2)), jnp.pad(bits[2:4], (0, 2))]
    ).astype(jnp.int32)

    across = [[site * PLANES + plane for site in range(SITES)] for plane in range(PLANES)]
    tiles = pltpu.with_memory_space_constraint(grm_tiles, pltpu.HBM)
    size = panel.shape[0] // SITES
    pieces = lax.all_to_all(
        panel.reshape(SITES, size, lanes), "col", 0, 0, axis_index_groups=across
    )
    keep, send = row_products(info, tiles, panel)
    pieces, keep, send = lax.optimization_barrier((pieces, keep, send))
    half = keep.shape[0] // 2
    share = half // SITES
    mine, send_z = small_call(
        add_kernel, [floats(half, lanes), coded(half, lanes)], keep, swap(send, "col", 1)
    )
    piece = pieces[owners[0] // PLANES]
    outs = [jax.ShapeDtypeStruct((size, lanes), panel.dtype)]
    piece = small_call(select_kernel, outs, bits, piece, swap(piece, "col", 1), scalars=1)[0]
    packed = small_call(
        pack_kernel,
        [jax.ShapeDtypeStruct((SITES, size, lanes), jnp.bfloat16)],
        bits, piece, swap(piece, "col", 2),
        scalars=1,
    )[0]
    slab = lax.all_to_all(packed, "col", 0, 0, axis_index_groups=across)
    got_z = swap(send_z, "col", 2)
    keep, *sends = col_products(info, tiles, slab, got_z)
    y_cols, begun = sum_over_row(bits, keep, sends)
    rows = small_call(rows_kernel, [floats(half, lanes)], mine, got_z, begun)[0]
    terms = lax.all_to_all(
        rows.reshape(SITES, share, lanes), "col", 0, 0, axis_index_groups=across
    )
    y_rows = small_call(total_kernel, [floats(share, lanes)], terms)[0]
    return (y_rows, y_cols)


def solution(mesh):
    in_specs = (P(("row", "col"), None, None), P(("row", "col")), P(("row", "col")), P("col", None))
    out_specs = (P(("row", "col"), None), P("col", None))
    return jax.shard_map(
        on_device, mesh=mesh, in_specs=in_specs, out_specs=out_specs, check_vma=False
    )
```

```python
import functools

import jax
import jax.numpy as jnp
from jax import lax
from jax.experimental import pallas as pl
from jax.experimental.pallas import tpu as pltpu
from jax.sharding import PartitionSpec as P

RT_DEV = 2
CTD = 2
STEPS = 2
MIB = 1024 * 1024
PAD = 16
SITES = 16
PLANES = 4
BF16_MOST = 3.3895313892515355e38


def place_of(info, index, depth, width):
    slot = index // STEPS
    part = index % STEPS
    local_row = info[0, slot]
    local_col = info[1, slot]
    first = pl.multiple_of(local_row * width + part * depth, depth)
    rows = pl.ds(first, depth)
    cols = pl.ds(pl.multiple_of(local_col * width, width), width)
    piece = pl.ds(pl.multiple_of(part * depth, depth), depth)
    return slot, part, rows, cols, piece


def fetch_of(info, tiles_ref, held, sems):
    slots, width, _ = held.shape
    depth = width // STEPS

    def fetch(index):
        slot, part, rows, cols, piece = place_of(info, index, depth, width)
        return pltpu.make_async_copy(
            tiles_ref.at[slot, piece], held.at[slot, piece], sems.at[index]
        )

    return fetch


def row_kernel(info, tiles_ref, panel_ref, keep_ref, send_ref, total, held, sems):
    slots, width, _ = held.shape
    depth = width // STEPS
    fetch = fetch_of(info, tiles_ref, held, sems)
    for index in range(slots * STEPS):
        fetch(index).start()
    total[...] = jnp.zeros_like(total)

    @pl.loop(0, slots * STEPS)
    def _(index):
        slot, part, rows, cols, piece = place_of(info, index, depth, width)
        kind = info[2, slot]
        fetch(index).wait()

        @pl.when(kind == 1)
        def _():
            total[rows, :] += jnp.dot(
                held[slot, piece, :], panel_ref[cols, :], preferred_element_type=jnp.float32
            )

        @pl.when(kind == 2)
        def _():
            row_ids = lax.broadcasted_iota(jnp.int32, (depth, width), 0) + part * depth
            col_ids = lax.broadcasted_iota(jnp.int32, (depth, width), 1)
            tile = held[slot, piece, :].astype(jnp.float32)
            lower = jnp.where(row_ids >= col_ids, tile, 0.0).astype(jnp.bfloat16)
            strict = jnp.where(row_ids > col_ids, tile, 0.0).astype(jnp.bfloat16)
            total[rows, :] += jnp.dot(lower, panel_ref[cols, :], preferred_element_type=jnp.float32)
            own = pl.ds(pl.multiple_of(info[1, slot] * width + part * depth, depth), depth)
            whole = pl.ds(pl.multiple_of(info[0, slot] * width, width), width)
            total[whole, :] += lax.dot_general(
                panel_ref[own, :], strict, (((0,), (0,)), ((), ())),
                preferred_element_type=jnp.float32,
            ).T

    core = info[4, 0]
    depth_z = info[4, 1]
    share = total.shape[0] // (SITES * PLANES)
    for ref, which in ((keep_ref, core), (send_ref, 1 - core)):
        for step, chip in enumerate((depth_z, 1 - depth_z)):
            for site in range(SITES):
                source = pl.multiple_of((site * PLANES + chip * 2 + which) * share, share)
                target = (step * SITES + site) * share
                ref[target : target + share, :] = total[pl.ds(source, share), :]


def add_kernel(keep_ref, got_ref, mine_ref, send_ref):
    size = mine_ref.shape[0]
    mine_ref[...] = keep_ref[:size, :] + got_ref[:size, :]
    encode(keep_ref[size:, :] + got_ref[size:, :], send_ref)


def pack_kernel(bits, pieces_ref, out_ref):
    piece = pieces_ref[bits[4]]
    for index in range(out_ref.shape[0]):
        out_ref[index] = piece


def rows_kernel(mine_ref, got_ref, after_ref, out_ref):
    del after_ref
    out_ref[...] = mine_ref[...] + decode(got_ref)


def total_kernel(terms_ref, out_ref):
    total = terms_ref[0]
    for site in range(1, terms_ref.shape[0]):
        total += terms_ref[site]
    out_ref[...] = total


def block_rows(size):
    return min(128, size)


def encode(value, out_ref):
    size = value.shape[0]
    block = block_rows(size)
    lanes = value.shape[1]
    powers = []
    for start in range(0, size, block):
        part = value[start : start + block]
        most = jnp.max(jnp.abs(part), axis=0, keepdims=True)
        power = 15.0 - jnp.maximum(jnp.ceil(jnp.log2(most)), -126.0)
        half = jnp.floor(power * 0.5)
        scaled = part * jnp.exp2(half) * jnp.exp2(power - half)
        whole = jnp.clip(jnp.round(scaled), -32767.0, 32767.0)
        out_ref[start : start + block, :] = whole.astype(jnp.int32).astype(jnp.int16)
        powers.append(power)
    powers.append(jnp.zeros((PAD - len(powers), lanes), jnp.float32))
    tail = jnp.concatenate(powers, axis=0)
    out_ref[size:, :] = tail.astype(jnp.int32).astype(jnp.int16)


def decode(ref):
    size = ref.shape[0] - PAD
    block = block_rows(size)
    tail = ref[size:, :].astype(jnp.int32).astype(jnp.float32)
    parts = []
    for index in range(size // block):
        power = tail[index : index + 1]
        half = jnp.floor(power * 0.5)
        part = ref[index * block : (index + 1) * block, :].astype(jnp.int32).astype(jnp.float32)
        parts.append(part * jnp.exp2(-half) * jnp.exp2(half - power))
    return jnp.concatenate(parts, axis=0)


def col_kernel(
    info, tiles_ref, near_ref, far_ref, keep_ref, send0_ref, send1_ref, slab, total, result, held, sems
):
    slots, width, _ = held.shape
    depth = width // STEPS
    fetch = fetch_of(info, tiles_ref, held, sems)
    for index in range(slots * STEPS):
        fetch(index).start()
    total[...] = jnp.zeros_like(total)
    core = info[4, 0]
    for ref, tile in ((near_ref, core), (far_ref, 1 - core)):
        rows = pl.ds(pl.multiple_of(tile * width, width), width)
        slab[rows, :] = ref[...].reshape(width, slab.shape[1])

    @pl.loop(0, slots * STEPS)
    def _(index):
        slot, part, rows, cols, piece = place_of(info, index, depth, width)
        fetch(index).wait()

        @pl.when(info[2, slot] == 1)
        def _():
            total[:, cols] += lax.dot_general(
                slab[rows, :], held[slot, piece, :], (((0,), (0,)), ((), ())),
                preferred_element_type=jnp.float32,
            )

    result[...] = total[...].T
    half = width // 2
    for index, send_ref in enumerate((send0_ref, send1_ref)):
        bit = info[3, index]
        mine = pl.multiple_of(index * width + bit * half, half)
        other = pl.multiple_of(index * width + (1 - bit) * half, half)
        keep_ref[index] = result[pl.ds(mine, half), :]
        encode(result[pl.ds(other, half), :], send_ref)


def first_kernel(index, keep_ref, got_ref, out_ref):
    encode(keep_ref[index] + decode(got_ref), out_ref)


def second_kernel(own_ref, got_ref, out_ref):
    encode(decode(own_ref) + decode(got_ref), out_ref)


def place_kernel(index, bits, own_ref, got_ref, *refs):
    out_ref, held, sem = refs[-3:]
    size = own_ref.shape[0] - PAD
    mine = pl.multiple_of(bits[index] * size, size)
    other = pl.multiple_of((1 - bits[index]) * size, size)
    held[pl.ds(mine, size), :] = decode(own_ref)
    held[pl.ds(other, size), :] = decode(got_ref)
    copy = pltpu.make_async_copy(held, out_ref.at[pl.ds(index * 2 * size, 2 * size)], sem)
    copy.start()
    copy.wait()


VMEM = pl.BlockSpec(memory_space=pltpu.VMEM)
SMEM = pl.BlockSpec(memory_space=pltpu.SMEM)
HBM = pl.BlockSpec(memory_space=pltpu.HBM)


def limit(size):
    return pltpu.CompilerParams(vmem_limit_bytes=size * MIB)


def small_call(kernel, outs, *args, scalars=0):
    return pl.pallas_call(
        kernel,
        in_specs=[SMEM] * scalars + [VMEM] * (len(args) - scalars),
        out_specs=[VMEM] * len(outs),
        out_shape=outs,
        compiler_params=limit(6),
    )(*args)


def place_half(index, bits, own, got, result):
    size, lanes = own.shape[0] - PAD, own.shape[1]
    args = (bits, own, got) + (() if result is None else (result,))
    return pl.pallas_call(
        functools.partial(place_kernel, index),
        in_specs=[SMEM, VMEM, VMEM] + [HBM] * (len(args) - 3),
        out_specs=HBM,
        out_shape=floats(4 * size, lanes),
        scratch_shapes=[pltpu.VMEM((2 * size, lanes), jnp.float32), pltpu.SemaphoreType.DMA],
        input_output_aliases={} if result is None else {3: 0},
        compiler_params=limit(6),
    )(*args)


def tile_cost(shape, lanes):
    slots, width, _ = shape
    return pl.CostEstimate(
        flops=2 * slots * width * width * lanes,
        bytes_accessed=2 * slots * width * width + 2 * MIB,
        transcendentals=0,
    )


def floats(*shape):
    return jax.ShapeDtypeStruct(shape, jnp.float32)


def coded(size, lanes):
    return jax.ShapeDtypeStruct((size + PAD, lanes), jnp.int16)


def tile_scratch(grm_tiles):
    return [
        pltpu.VMEM(grm_tiles.shape, grm_tiles.dtype),
        pltpu.SemaphoreType.DMA((grm_tiles.shape[0] * STEPS,)),
    ]


def row_products(info, grm_tiles, panel):
    slots, width, _ = grm_tiles.shape
    lanes = panel.shape[1]
    rows = RT_DEV * width
    return pl.pallas_call(
        row_kernel,
        in_specs=[SMEM, HBM, VMEM],
        out_specs=[VMEM, VMEM],
        out_shape=[floats(rows // 2, lanes), floats(rows // 2, lanes)],
        scratch_shapes=[pltpu.VMEM((rows, lanes), jnp.float32)] + tile_scratch(grm_tiles),
        compiler_params=limit(24),
        cost_estimate=tile_cost(grm_tiles.shape, lanes),
    )(info, grm_tiles, panel)


def col_products(info, grm_tiles, near, far):
    slots, width, _ = grm_tiles.shape
    lanes = near.shape[2]
    half = width // 2
    return pl.pallas_call(
        col_kernel,
        in_specs=[SMEM, HBM, VMEM, VMEM],
        out_specs=[VMEM] * 3,
        out_shape=[floats(2, half, lanes), coded(half, lanes), coded(half, lanes)],
        scratch_shapes=[
            pltpu.VMEM((RT_DEV * width, lanes), near.dtype),
            pltpu.VMEM((lanes, CTD * width), jnp.float32),
            pltpu.VMEM((CTD * width, lanes), jnp.float32),
        ]
        + tile_scratch(grm_tiles),
        compiler_params=limit(24),
        cost_estimate=tile_cost(grm_tiles.shape, lanes),
    )(info, grm_tiles, near, far)


def swap(value, axis, flip):
    return lax.ppermute(value, axis, [(k, k ^ flip) for k in range(lax.axis_size(axis))])


def sum_over_row(bits, keep, sends):
    size, lanes = keep.shape[1:]
    outs = [coded(size, lanes)]
    flips = [(1, 3, 1), (3, 1, 3)]
    gots = [swap(send, "row", flip[0]) for send, flip in zip(sends, flips)]
    owns = [
        small_call(functools.partial(first_kernel, index), outs, keep, got)[0]
        for index, got in enumerate(gots)
    ]
    begun = owns[0]
    gots = [swap(own, "row", flip[1]) for own, flip in zip(owns, flips)]
    owns = [small_call(second_kernel, outs, own, got)[0] for own, got in zip(owns, gots)]
    gots = [swap(own, "row", flip[2]) for own, flip in zip(owns, flips)]
    result = None
    for index in range(2):
        result = place_half(index, bits, owns[index], gots[index], result)
    return result, begun


def on_device(grm_tiles, tile_row, tile_col, panel):
    row_index = lax.axis_index("row")
    col_index = lax.axis_index("col")
    col_count = lax.axis_size("col")
    row_count = lax.axis_size("row")
    lanes = panel.shape[1]
    offset = CTD * col_count - RT_DEV * row_count
    base_row = row_index * RT_DEV
    base_col = col_index * CTD
    owners = [(offset + row * RT_DEV) // CTD for row in range(row_count)]

    local_row = tile_row - base_row
    local_col = jnp.maximum(tile_col - base_col, 0)
    kind = jnp.where(tile_col < 0, 0, jnp.where(tile_col == offset + tile_row, 2, 1))
    high = row_index // 2
    low = (row_index + high) % 2
    core = col_index % 2
    chip = col_index // 2 % 2
    root = (offset + base_row) // CTD
    chips = col_count // 2
    bits = jnp.stack([low, high, core, chip, root % 2 * chips + root // 2]).astype(jnp.int32)
    info = jnp.stack(
        [local_row, local_col, kind, jnp.pad(bits[:2], (0, 2)), jnp.pad(bits[2:4], (0, 2))]
    ).astype(jnp.int32)

    across = [[site * PLANES + plane for site in range(SITES)] for plane in range(PLANES)]
    tiles = pltpu.with_memory_space_constraint(grm_tiles, pltpu.HBM)
    one_core = [[chip * 2 + core for chip in range(chips)] for core in range(2)]
    size = panel.shape[0] // col_count
    pieces = lax.all_to_all(
        panel.reshape(col_count, size, lanes), "col", 0, 0,
        axis_index_groups=[one_core[0] + one_core[1]],
    )
    keep, send = row_products(info, tiles, panel)
    pieces, keep, send = lax.optimization_barrier((pieces, keep, send))
    half = keep.shape[0] // 2
    share = half // SITES
    mine, send_z = small_call(
        add_kernel, [floats(half, lanes), coded(half, lanes)], keep, swap(send, "col", 1)
    )
    packed = small_call(
        pack_kernel,
        [jax.ShapeDtypeStruct((chips, size, lanes), panel.dtype)],
        bits, pieces,
        scalars=1,
    )[0]
    near = lax.all_to_all(packed, "col", 0, 0, axis_index_groups=one_core)
    near, got_z = lax.optimization_barrier((near, swap(send_z, "col", 2)))
    far = swap(near, "col", 1)
    keep, *sends = col_products(info, tiles, near, far)
    y_cols, begun = sum_over_row(bits, keep, sends)
    rows = small_call(rows_kernel, [floats(half, lanes)], mine, got_z, begun)[0]
    terms = lax.all_to_all(
        rows.reshape(SITES, share, lanes), "col", 0, 0, axis_index_groups=across
    )
    y_rows = small_call(total_kernel, [floats(share, lanes)], terms)[0]
    return (y_rows, y_cols)


def solution(mesh):
    in_specs = (P(("row", "col"), None, None), P(("row", "col")), P(("row", "col")), P("col", None))
    out_specs = (P(("row", "col"), None), P("col", None))
    return jax.shard_map(
        on_device, mesh=mesh, in_specs=in_specs, out_specs=out_specs, check_vma=False
    )
```

```python
import functools

import jax
import jax.numpy as jnp
from jax import lax
from jax.experimental import pallas as pl
from jax.experimental.pallas import tpu as pltpu
from jax.sharding import PartitionSpec as P

RT_DEV = 2
CTD = 2
STEPS = 2
MIB = 1024 * 1024
PAD = 16
SITES = 16
PLANES = 4
BF16_MOST = 3.3895313892515355e38


def place_of(info, index, depth, width):
    slot = index // STEPS
    part = index % STEPS
    local_row = info[0, slot]
    local_col = info[1, slot]
    first = pl.multiple_of(local_row * width + part * depth, depth)
    rows = pl.ds(first, depth)
    cols = pl.ds(pl.multiple_of(local_col * width, width), width)
    piece = pl.ds(pl.multiple_of(part * depth, depth), depth)
    return slot, part, rows, cols, piece


def fetch_of(info, tiles_ref, held, sems):
    slots, width, _ = held.shape
    depth = width // STEPS

    def fetch(index):
        slot, part, rows, cols, piece = place_of(info, index, depth, width)
        return pltpu.make_async_copy(
            tiles_ref.at[slot, piece], held.at[slot, piece], sems.at[index]
        )

    return fetch


def row_kernel(info, tiles_ref, panel_ref, keep_ref, send_ref, total, held, sems):
    slots, width, _ = held.shape
    depth = width // STEPS
    fetch = fetch_of(info, tiles_ref, held, sems)
    for index in range(slots * STEPS):
        fetch(index).start()
    total[...] = jnp.zeros_like(total)

    @pl.loop(0, slots * STEPS)
    def _(index):
        slot, part, rows, cols, piece = place_of(info, index, depth, width)
        kind = info[2, slot]
        fetch(index).wait()

        @pl.when(kind == 1)
        def _():
            total[rows, :] += jnp.dot(
                held[slot, piece, :], panel_ref[cols, :], preferred_element_type=jnp.float32
            )

        @pl.when(kind == 2)
        def _():
            row_ids = lax.broadcasted_iota(jnp.int32, (depth, width), 0) + part * depth
            col_ids = lax.broadcasted_iota(jnp.int32, (depth, width), 1)
            tile = held[slot, piece, :].astype(jnp.float32)
            lower = jnp.where(row_ids >= col_ids, tile, 0.0).astype(jnp.bfloat16)
            strict = jnp.where(row_ids > col_ids, tile, 0.0).astype(jnp.bfloat16)
            total[rows, :] += jnp.dot(lower, panel_ref[cols, :], preferred_element_type=jnp.float32)
            own = pl.ds(pl.multiple_of(info[1, slot] * width + part * depth, depth), depth)
            whole = pl.ds(pl.multiple_of(info[0, slot] * width, width), width)
            total[whole, :] += lax.dot_general(
                panel_ref[own, :], strict, (((0,), (0,)), ((), ())),
                preferred_element_type=jnp.float32,
            ).T

    core = info[4, 0]
    depth_z = info[4, 1]
    share = total.shape[0] // (SITES * PLANES)
    for ref, which in ((keep_ref, core), (send_ref, 1 - core)):
        for step, chip in enumerate((depth_z, 1 - depth_z)):
            for site in range(SITES):
                source = pl.multiple_of((site * PLANES + chip * 2 + which) * share, share)
                target = (step * SITES + site) * share
                ref[target : target + share, :] = total[pl.ds(source, share), :]


def add_kernel(keep_ref, got_ref, mine_ref, send_ref):
    size = mine_ref.shape[0]
    mine_ref[...] = keep_ref[:size, :] + got_ref[:size, :]
    encode(keep_ref[size:, :] + got_ref[size:, :], send_ref)


def rows_kernel(mine_ref, got_ref, after_ref, out_ref):
    del after_ref
    out_ref[...] = mine_ref[...] + decode(got_ref)


def total_kernel(terms_ref, out_ref):
    total = terms_ref[0]
    for site in range(1, terms_ref.shape[0]):
        total += terms_ref[site]
    out_ref[...] = total


def block_rows(size):
    return min(128, size)


def encode(value, out_ref):
    size = value.shape[0]
    block = block_rows(size)
    lanes = value.shape[1]
    powers = []
    for start in range(0, size, block):
        part = value[start : start + block]
        most = jnp.max(jnp.abs(part), axis=0, keepdims=True)
        power = 15.0 - jnp.maximum(jnp.ceil(jnp.log2(most)), -126.0)
        half = jnp.floor(power * 0.5)
        scaled = part * jnp.exp2(half) * jnp.exp2(power - half)
        whole = jnp.clip(jnp.round(scaled), -32767.0, 32767.0)
        out_ref[start : start + block, :] = whole.astype(jnp.int32).astype(jnp.int16)
        powers.append(power)
    powers.append(jnp.zeros((PAD - len(powers), lanes), jnp.float32))
    tail = jnp.concatenate(powers, axis=0)
    out_ref[size:, :] = tail.astype(jnp.int32).astype(jnp.int16)


def decode(ref):
    size = ref.shape[0] - PAD
    block = block_rows(size)
    tail = ref[size:, :].astype(jnp.int32).astype(jnp.float32)
    parts = []
    for index in range(size // block):
        power = tail[index : index + 1]
        half = jnp.floor(power * 0.5)
        part = ref[index * block : (index + 1) * block, :].astype(jnp.int32).astype(jnp.float32)
        parts.append(part * jnp.exp2(-half) * jnp.exp2(half - power))
    return jnp.concatenate(parts, axis=0)


def col_kernel(
    info, tiles_ref, near_ref, far_ref, keep_ref, send0_ref, send1_ref, slab, total, result, held, sems
):
    slots, width, _ = held.shape
    depth = width // STEPS
    fetch = fetch_of(info, tiles_ref, held, sems)
    for index in range(slots * STEPS):
        fetch(index).start()
    total[...] = jnp.zeros_like(total)
    core = info[4, 0]
    for ref, tile in ((near_ref, core), (far_ref, 1 - core)):
        rows = pl.ds(pl.multiple_of(tile * width, width), width)
        slab[rows, :] = ref[...].reshape(width, slab.shape[1])

    @pl.loop(0, slots * STEPS)
    def _(index):
        slot, part, rows, cols, piece = place_of(info, index, depth, width)
        fetch(index).wait()

        @pl.when(info[2, slot] == 1)
        def _():
            total[:, cols] += lax.dot_general(
                slab[rows, :], held[slot, piece, :], (((0,), (0,)), ((), ())),
                preferred_element_type=jnp.float32,
            )

    result[...] = total[...].T
    half = width // 2
    for index, send_ref in enumerate((send0_ref, send1_ref)):
        bit = info[3, index]
        mine = pl.multiple_of(index * width + bit * half, half)
        other = pl.multiple_of(index * width + (1 - bit) * half, half)
        keep_ref[index] = result[pl.ds(mine, half), :]
        encode(result[pl.ds(other, half), :], send_ref)


def first_kernel(index, keep_ref, got_ref, out_ref):
    encode(keep_ref[index] + decode(got_ref), out_ref)


def second_kernel(own_ref, got_ref, out_ref):
    encode(decode(own_ref) + decode(got_ref), out_ref)


def place_kernel(index, far, bits, half_ref, *refs):
    out_ref, held, sem = refs[-3:]
    size = held.shape[0]
    held[...] = decode(half_ref)
    side = 1 - bits[index] if far else bits[index]
    first = pl.multiple_of((index * 2 + side) * size, size)
    copy = pltpu.make_async_copy(held, out_ref.at[pl.ds(first, size)], sem)
    copy.start()
    copy.wait()


VMEM = pl.BlockSpec(memory_space=pltpu.VMEM)
SMEM = pl.BlockSpec(memory_space=pltpu.SMEM)
HBM = pl.BlockSpec(memory_space=pltpu.HBM)


def limit(size):
    return pltpu.CompilerParams(vmem_limit_bytes=size * MIB)


def small_call(kernel, outs, *args, scalars=0):
    return pl.pallas_call(
        kernel,
        in_specs=[SMEM] * scalars + [VMEM] * (len(args) - scalars),
        out_specs=[VMEM] * len(outs),
        out_shape=outs,
        compiler_params=limit(6),
    )(*args)


def place_half(index, far, bits, half, result):
    size, lanes = half.shape[0] - PAD, half.shape[1]
    args = (bits, half) + (() if result is None else (result,))
    return pl.pallas_call(
        functools.partial(place_kernel, index, far),
        in_specs=[SMEM, VMEM] + [HBM] * (len(args) - 2),
        out_specs=HBM,
        out_shape=floats(4 * size, lanes),
        scratch_shapes=[pltpu.VMEM((size, lanes), jnp.float32), pltpu.SemaphoreType.DMA],
        input_output_aliases={} if result is None else {2: 0},
        compiler_params=limit(6),
    )(*args)


def tile_cost(shape, lanes):
    slots, width, _ = shape
    return pl.CostEstimate(
        flops=2 * slots * width * width * lanes,
        bytes_accessed=2 * slots * width * width + 2 * MIB,
        transcendentals=0,
    )


def floats(*shape):
    return jax.ShapeDtypeStruct(shape, jnp.float32)


def coded(size, lanes):
    return jax.ShapeDtypeStruct((size + PAD, lanes), jnp.int16)


def tile_scratch(grm_tiles):
    return [
        pltpu.VMEM(grm_tiles.shape, grm_tiles.dtype),
        pltpu.SemaphoreType.DMA((grm_tiles.shape[0] * STEPS,)),
    ]


def row_products(info, grm_tiles, panel):
    slots, width, _ = grm_tiles.shape
    lanes = panel.shape[1]
    rows = RT_DEV * width
    return pl.pallas_call(
        row_kernel,
        in_specs=[SMEM, HBM, VMEM],
        out_specs=[VMEM, VMEM],
        out_shape=[floats(rows // 2, lanes), floats(rows // 2, lanes)],
        scratch_shapes=[pltpu.VMEM((rows, lanes), jnp.float32)] + tile_scratch(grm_tiles),
        compiler_params=limit(24),
        cost_estimate=tile_cost(grm_tiles.shape, lanes),
    )(info, grm_tiles, panel)


def col_products(info, grm_tiles, near, far):
    slots, width, _ = grm_tiles.shape
    lanes = near.shape[2]
    half = width // 2
    return pl.pallas_call(
        col_kernel,
        in_specs=[SMEM, HBM, VMEM, VMEM],
        out_specs=[VMEM] * 3,
        out_shape=[floats(2, half, lanes), coded(half, lanes), coded(half, lanes)],
        scratch_shapes=[
            pltpu.VMEM((RT_DEV * width, lanes), near.dtype),
            pltpu.VMEM((lanes, CTD * width), jnp.float32),
            pltpu.VMEM((CTD * width, lanes), jnp.float32),
        ]
        + tile_scratch(grm_tiles),
        compiler_params=limit(24),
        cost_estimate=tile_cost(grm_tiles.shape, lanes),
    )(info, grm_tiles, near, far)


def swap(value, axis, flip):
    return lax.ppermute(value, axis, [(k, k ^ flip) for k in range(lax.axis_size(axis))])


def sum_over_row(bits, keep, sends):
    size, lanes = keep.shape[1:]
    outs = [coded(size, lanes)]
    flips = [(1, 3, 1), (3, 1, 3)]
    gots = [swap(send, "row", flip[0]) for send, flip in zip(sends, flips)]
    owns = [
        small_call(functools.partial(first_kernel, index), outs, keep, got)[0]
        for index, got in enumerate(gots)
    ]
    begun = owns[0]
    gots = [swap(own, "row", flip[1]) for own, flip in zip(owns, flips)]
    owns = [small_call(second_kernel, outs, own, got)[0] for own, got in zip(owns, gots)]
    gots = [swap(own, "row", flip[2]) for own, flip in zip(owns, flips)]
    result = None
    for far, halves in enumerate((owns, gots)):
        for index, half in enumerate(halves):
            result = place_half(index, far, bits, half, result)
    return result, begun


def on_device(grm_tiles, tile_row, tile_col, panel):
    row_index = lax.axis_index("row")
    col_index = lax.axis_index("col")
    col_count = lax.axis_size("col")
    row_count = lax.axis_size("row")
    lanes = panel.shape[1]
    offset = CTD * col_count - RT_DEV * row_count
    base_row = row_index * RT_DEV
    base_col = col_index * CTD
    owners = [(offset + row * RT_DEV) // CTD for row in range(row_count)]

    local_row = tile_row - base_row
    local_col = jnp.maximum(tile_col - base_col, 0)
    kind = jnp.where(tile_col < 0, 0, jnp.where(tile_col == offset + tile_row, 2, 1))
    high = row_index // 2
    low = (row_index + high) % 2
    core = col_index % 2
    chip = col_index // 2 % 2
    root = (offset + base_row) // CTD
    chips = col_count // 2
    bits = jnp.stack([low, high, core, chip]).astype(jnp.int32)
    info = jnp.stack(
        [local_row, local_col, kind, jnp.pad(bits[:2], (0, 2)), jnp.pad(bits[2:4], (0, 2))]
    ).astype(jnp.int32)

    across = [[site * PLANES + plane for site in range(SITES)] for plane in range(PLANES)]
    tiles = pltpu.with_memory_space_constraint(grm_tiles, pltpu.HBM)
    one_core = [[chip * 2 + core for chip in range(chips)] for core in range(2)]
    size = panel.shape[0] // col_count
    pieces = lax.all_to_all(
        panel.reshape(col_count, size, lanes), "col", 0, 0,
        axis_index_groups=[one_core[0] + one_core[1]],
    )
    keep, send = row_products(info, tiles, panel)
    pieces, keep, send = lax.optimization_barrier((pieces, keep, send))
    half = keep.shape[0] // 2
    share = half // SITES
    mine, send_z = small_call(
        add_kernel, [floats(half, lanes), coded(half, lanes)], keep, swap(send, "col", 1)
    )
    place = root % 2 * chips + root // 2
    piece = lax.dynamic_index_in_dim(pieces, place, 0)
    packed = jnp.broadcast_to(piece, (chips, size, lanes))
    near = lax.all_to_all(packed, "col", 0, 0, axis_index_groups=one_core)
    near, got_z = lax.optimization_barrier((near, swap(send_z, "col", 2)))
    far = swap(near, "col", 1)
    keep, *sends = col_products(info, tiles, near, far)
    y_cols, begun = sum_over_row(bits, keep, sends)
    rows = small_call(rows_kernel, [floats(half, lanes)], mine, got_z, begun)[0]
    terms = lax.all_to_all(
        rows.reshape(SITES, share, lanes), "col", 0, 0, axis_index_groups=across
    )
    y_rows = small_call(total_kernel, [floats(share, lanes)], terms)[0]
    return (y_rows, y_cols)


def solution(mesh):
    in_specs = (P(("row", "col"), None, None), P(("row", "col")), P(("row", "col")), P("col", None))
    out_specs = (P(("row", "col"), None), P("col", None))
    return jax.shard_map(
        on_device, mesh=mesh, in_specs=in_specs, out_specs=out_specs, check_vma=False
    )
```

```python
import functools

import jax
import jax.numpy as jnp
from jax import lax
from jax.experimental import pallas as pl
from jax.experimental.pallas import tpu as pltpu
from jax.sharding import PartitionSpec as P

RT_DEV = 2
CTD = 2
STEPS = 2
MIB = 1024 * 1024
PAD = 16
SITES = 16
PLANES = 4
BF16_MOST = 3.3895313892515355e38


def place_of(info, index, depth, width):
    slot = index // STEPS
    part = index % STEPS
    local_row = info[0, slot]
    local_col = info[1, slot]
    first = pl.multiple_of(local_row * width + part * depth, depth)
    rows = pl.ds(first, depth)
    cols = pl.ds(pl.multiple_of(local_col * width, width), width)
    piece = pl.ds(pl.multiple_of(part * depth, depth), depth)
    return slot, part, rows, cols, piece


def fetch_of(info, tiles_ref, held, sems):
    slots, width, _ = held.shape
    depth = width // STEPS

    def fetch(index):
        slot, part, rows, cols, piece = place_of(info, index, depth, width)
        return pltpu.make_async_copy(
            tiles_ref.at[slot, piece], held.at[slot, piece], sems.at[index]
        )

    return fetch


def row_kernel(info, tiles_ref, panel_ref, keep_ref, send_ref, total, held, sems):
    slots, width, _ = held.shape
    depth = width // STEPS
    fetch = fetch_of(info, tiles_ref, held, sems)
    for index in range(slots * STEPS):
        fetch(index).start()
    total[...] = jnp.zeros_like(total)

    @pl.loop(0, slots * STEPS)
    def _(index):
        slot, part, rows, cols, piece = place_of(info, index, depth, width)
        kind = info[2, slot]
        fetch(index).wait()

        @pl.when(kind == 1)
        def _():
            total[rows, :] += jnp.dot(
                held[slot, piece, :], panel_ref[cols, :], preferred_element_type=jnp.float32
            )

        @pl.when(kind == 2)
        def _():
            row_ids = lax.broadcasted_iota(jnp.int32, (depth, width), 0) + part * depth
            col_ids = lax.broadcasted_iota(jnp.int32, (depth, width), 1)
            tile = held[slot, piece, :].astype(jnp.float32)
            lower = jnp.where(row_ids >= col_ids, tile, 0.0).astype(jnp.bfloat16)
            strict = jnp.where(row_ids > col_ids, tile, 0.0).astype(jnp.bfloat16)
            total[rows, :] += jnp.dot(lower, panel_ref[cols, :], preferred_element_type=jnp.float32)
            own = pl.ds(pl.multiple_of(info[1, slot] * width + part * depth, depth), depth)
            whole = pl.ds(pl.multiple_of(info[0, slot] * width, width), width)
            total[whole, :] += lax.dot_general(
                panel_ref[own, :], strict, (((0,), (0,)), ((), ())),
                preferred_element_type=jnp.float32,
            ).T

    core = info[4, 0]
    depth_z = info[4, 1]
    share = total.shape[0] // (SITES * PLANES)
    for ref, which in ((keep_ref, core), (send_ref, 1 - core)):
        for step, chip in enumerate((depth_z, 1 - depth_z)):
            for site in range(SITES):
                source = pl.multiple_of((site * PLANES + chip * 2 + which) * share, share)
                target = (step * SITES + site) * share
                ref[target : target + share, :] = total[pl.ds(source, share), :]


def add_kernel(keep_ref, got_ref, mine_ref, send_ref):
    size = mine_ref.shape[0]
    mine_ref[...] = keep_ref[:size, :] + got_ref[:size, :]
    encode(keep_ref[size:, :] + got_ref[size:, :], send_ref)


def rows_kernel(mine_ref, got_ref, after_ref, out_ref):
    del after_ref
    out_ref[...] = mine_ref[...] + decode(got_ref)


def block_rows(size):
    return min(128, size)


def encode(value, out_ref):
    size = value.shape[0]
    block = block_rows(size)
    lanes = value.shape[1]
    powers = []
    for start in range(0, size, block):
        part = value[start : start + block]
        most = jnp.max(jnp.abs(part), axis=0, keepdims=True)
        power = 15.0 - jnp.maximum(jnp.ceil(jnp.log2(most)), -126.0)
        half = jnp.floor(power * 0.5)
        scaled = part * jnp.exp2(half) * jnp.exp2(power - half)
        whole = jnp.clip(jnp.round(scaled), -32767.0, 32767.0)
        out_ref[start : start + block, :] = whole.astype(jnp.int32).astype(jnp.int16)
        powers.append(power)
    powers.append(jnp.zeros((PAD - len(powers), lanes), jnp.float32))
    tail = jnp.concatenate(powers, axis=0)
    out_ref[size:, :] = tail.astype(jnp.int32).astype(jnp.int16)


def decode(ref):
    size = ref.shape[0] - PAD
    block = block_rows(size)
    tail = ref[size:, :].astype(jnp.int32).astype(jnp.float32)
    parts = []
    for index in range(size // block):
        power = tail[index : index + 1]
        half = jnp.floor(power * 0.5)
        part = ref[index * block : (index + 1) * block, :].astype(jnp.int32).astype(jnp.float32)
        parts.append(part * jnp.exp2(-half) * jnp.exp2(half - power))
    return jnp.concatenate(parts, axis=0)


def fetch_kernel(tiles_ref, after_ref, held_ref, token_ref, sems):
    del after_ref
    slots, width, _ = held_ref.shape
    depth = width // STEPS
    copies = []
    for index in range(slots * STEPS):
        piece = pl.ds(index % STEPS * depth, depth)
        copies.append(
            pltpu.make_async_copy(
                tiles_ref.at[index // STEPS, piece],
                held_ref.at[index // STEPS, piece],
                sems.at[index],
            )
        )
    for copy in copies:
        copy.start()
    token_ref[...] = jnp.zeros_like(token_ref)
    for copy in copies:
        copy.wait()


def col_kernel(
    info, held, near_ref, far_ref, keep_ref, send0_ref, send1_ref, slab, total, result
):
    slots, width, _ = held.shape
    depth = width // STEPS
    total[...] = jnp.zeros_like(total)
    core = info[4, 0]
    for ref, tile in ((near_ref, core), (far_ref, 1 - core)):
        rows = pl.ds(pl.multiple_of(tile * width, width), width)
        slab[rows, :] = ref[...].reshape(width, slab.shape[1])

    @pl.loop(0, slots * STEPS)
    def _(index):
        slot, part, rows, cols, piece = place_of(info, index, depth, width)

        @pl.when(info[2, slot] == 1)
        def _():
            total[:, cols] += lax.dot_general(
                slab[rows, :], held[slot, piece, :], (((0,), (0,)), ((), ())),
                preferred_element_type=jnp.float32,
            )

    result[...] = total[...].T
    half = width // 2
    for index, send_ref in enumerate((send0_ref, send1_ref)):
        bit = info[3, index]
        mine = pl.multiple_of(index * width + bit * half, half)
        other = pl.multiple_of(index * width + (1 - bit) * half, half)
        keep_ref[index] = result[pl.ds(mine, half), :]
        encode(result[pl.ds(other, half), :], send_ref)


def first_kernel(index, keep_ref, got_ref, out_ref):
    encode(keep_ref[index] + decode(got_ref), out_ref)


def second_kernel(own_ref, got_ref, out_ref):
    encode(decode(own_ref) + decode(got_ref), out_ref)


def place_halves(far, half_refs, out_ref, held, sems):
    size = held.shape[1]
    row = lax.axis_index("row")
    high = row // 2
    copies = []
    for index, (half_ref, bit) in enumerate(zip(half_refs, ((row + high) % 2, high))):
        held[index] = decode(half_ref)
        side = 1 - bit if far else bit
        first = pl.multiple_of((index * 2 + side) * size, size)
        copy = pltpu.make_async_copy(
            held.at[index], out_ref.at[pl.ds(first, size)], sems.at[index]
        )
        copy.start()
        copies.append(copy)
    for copy in copies:
        copy.wait()


def own_kernel(half0_ref, half1_ref, out_ref, held, sems):
    place_halves(False, (half0_ref, half1_ref), out_ref, held, sems)


def last_kernel(half0_ref, half1_ref, terms_ref, result_ref, out_ref, rows_ref, held, sems):
    del result_ref
    total = terms_ref[0]
    for site in range(1, terms_ref.shape[0]):
        total += terms_ref[site]
    rows_ref[...] = total
    place_halves(True, (half0_ref, half1_ref), out_ref, held, sems)


VMEM = pl.BlockSpec(memory_space=pltpu.VMEM)
SMEM = pl.BlockSpec(memory_space=pltpu.SMEM)
HBM = pl.BlockSpec(memory_space=pltpu.HBM)


def limit(size):
    return pltpu.CompilerParams(vmem_limit_bytes=size * MIB)


def small_call(kernel, outs, *args, scalars=0):
    return pl.pallas_call(
        kernel,
        in_specs=[SMEM] * scalars + [VMEM] * (len(args) - scalars),
        out_specs=[VMEM] * len(outs),
        out_shape=outs,
        compiler_params=limit(6),
    )(*args)


def place_scratch(size, lanes):
    return [pltpu.VMEM((2, size, lanes), jnp.float32), pltpu.SemaphoreType.DMA((2,))]


def place_own(owns):
    size, lanes = owns[0].shape[0] - PAD, owns[0].shape[1]
    return pl.pallas_call(
        own_kernel,
        in_specs=[VMEM, VMEM],
        out_specs=HBM,
        out_shape=floats(4 * size, lanes),
        scratch_shapes=place_scratch(size, lanes),
        compiler_params=limit(6),
    )(*owns)


def place_last(gots, terms, result):
    size, lanes = gots[0].shape[0] - PAD, gots[0].shape[1]
    return pl.pallas_call(
        last_kernel,
        in_specs=[VMEM, VMEM, VMEM, HBM],
        out_specs=[HBM, VMEM],
        out_shape=[floats(4 * size, lanes), floats(*terms.shape[1:])],
        scratch_shapes=place_scratch(size, lanes),
        input_output_aliases={3: 0},
        compiler_params=limit(6),
    )(*gots, terms, result)


def tile_cost(shape, lanes):
    slots, width, _ = shape
    return pl.CostEstimate(
        flops=2 * slots * width * width * lanes,
        bytes_accessed=2 * slots * width * width + 2 * MIB,
        transcendentals=0,
    )


def floats(*shape):
    return jax.ShapeDtypeStruct(shape, jnp.float32)


def coded(size, lanes):
    return jax.ShapeDtypeStruct((size + PAD, lanes), jnp.int16)


def tile_scratch(grm_tiles):
    return [
        pltpu.VMEM(grm_tiles.shape, grm_tiles.dtype),
        pltpu.SemaphoreType.DMA((grm_tiles.shape[0] * STEPS,)),
    ]


def row_products(info, grm_tiles, panel):
    slots, width, _ = grm_tiles.shape
    lanes = panel.shape[1]
    rows = RT_DEV * width
    return pl.pallas_call(
        row_kernel,
        in_specs=[SMEM, HBM, VMEM],
        out_specs=[VMEM, VMEM],
        out_shape=[floats(rows // 2, lanes), floats(rows // 2, lanes)],
        scratch_shapes=[pltpu.VMEM((rows, lanes), jnp.float32)] + tile_scratch(grm_tiles),
        compiler_params=limit(24),
        cost_estimate=tile_cost(grm_tiles.shape, lanes),
    )(info, grm_tiles, panel)


def fetch_tiles(grm_tiles, after):
    return pl.pallas_call(
        fetch_kernel,
        in_specs=[HBM, VMEM],
        out_specs=[VMEM, VMEM],
        out_shape=[pltpu.VMEM(grm_tiles.shape, grm_tiles.dtype), floats(8, 128)],
        scratch_shapes=[pltpu.SemaphoreType.DMA((grm_tiles.shape[0] * STEPS,))],
        compiler_params=limit(12),
    )(grm_tiles, after)


def col_products(info, grm_tiles, near, far):
    slots, width, _ = grm_tiles.shape
    lanes = near.shape[2]
    half = width // 2
    return pl.pallas_call(
        col_kernel,
        in_specs=[SMEM, VMEM, VMEM, VMEM],
        out_specs=[VMEM] * 3,
        out_shape=[floats(2, half, lanes), coded(half, lanes), coded(half, lanes)],
        scratch_shapes=[
            pltpu.VMEM((RT_DEV * width, lanes), near.dtype),
            pltpu.VMEM((lanes, CTD * width), jnp.float32),
            pltpu.VMEM((CTD * width, lanes), jnp.float32),
        ],
        compiler_params=limit(24),
        cost_estimate=tile_cost(grm_tiles.shape, lanes),
    )(info, grm_tiles, near, far)


def swap(value, axis, flip):
    return lax.ppermute(value, axis, [(k, k ^ flip) for k in range(lax.axis_size(axis))])


def sum_over_row(keep, sends):
    size, lanes = keep.shape[1:]
    outs = [coded(size, lanes)]
    flips = [(1, 3, 1), (3, 1, 3)]
    gots = [swap(send, "row", flip[0]) for send, flip in zip(sends, flips)]
    owns = [
        small_call(functools.partial(first_kernel, index), outs, keep, got)[0]
        for index, got in enumerate(gots)
    ]
    begun = owns[0]
    gots = [swap(own, "row", flip[1]) for own, flip in zip(owns, flips)]
    owns = [small_call(second_kernel, outs, own, got)[0] for own, got in zip(owns, gots)]
    gots = [swap(own, "row", flip[2]) for own, flip in zip(owns, flips)]
    return gots, place_own(owns), begun


def on_device(grm_tiles, tile_row, tile_col, panel):
    row_index = lax.axis_index("row")
    col_index = lax.axis_index("col")
    col_count = lax.axis_size("col")
    row_count = lax.axis_size("row")
    lanes = panel.shape[1]
    offset = CTD * col_count - RT_DEV * row_count
    base_row = row_index * RT_DEV
    base_col = col_index * CTD
    owners = [(offset + row * RT_DEV) // CTD for row in range(row_count)]

    local_row = tile_row - base_row
    local_col = jnp.maximum(tile_col - base_col, 0)
    kind = jnp.where(tile_col < 0, 0, jnp.where(tile_col == offset + tile_row, 2, 1))
    high = row_index // 2
    low = (row_index + high) % 2
    core = col_index % 2
    chip = col_index // 2 % 2
    root = (offset + base_row) // CTD
    chips = col_count // 2
    bits = jnp.stack([low, high, core, chip]).astype(jnp.int32)
    info = jnp.stack(
        [local_row, local_col, kind, jnp.pad(bits[:2], (0, 2)), jnp.pad(bits[2:4], (0, 2))]
    ).astype(jnp.int32)

    across = [[site * PLANES + plane for site in range(SITES)] for plane in range(PLANES)]
    tiles = pltpu.with_memory_space_constraint(grm_tiles, pltpu.HBM)
    one_core = [[chip * 2 + core for chip in range(chips)] for core in range(2)]
    size = panel.shape[0] // col_count
    pieces = lax.all_to_all(
        panel.reshape(col_count, size, lanes), "col", 0, 0,
        axis_index_groups=[one_core[0] + one_core[1]],
    )
    keep, send = row_products(info, tiles, panel)
    pieces, keep, send = lax.optimization_barrier((pieces, keep, send))
    half = keep.shape[0] // 2
    share = half // SITES
    mine, send_z = small_call(
        add_kernel, [floats(half, lanes), coded(half, lanes)], keep, swap(send, "col", 1)
    )
    place = root % 2 * chips + root // 2
    piece = lax.dynamic_index_in_dim(pieces, place, 0)
    packed = jnp.broadcast_to(piece, (chips, size, lanes))
    near = lax.all_to_all(packed, "col", 0, 0, axis_index_groups=one_core)
    got_z = swap(send_z, "col", 2)
    held, token = fetch_tiles(tiles, send_z)
    near, got_z, token = lax.optimization_barrier((near, got_z, token))
    far = swap(near, "col", 1)
    keep, *sends = col_products(info, held, near, far)
    gots, result, begun = sum_over_row(keep, sends)
    rows = small_call(rows_kernel, [floats(half, lanes)], mine, got_z, begun)[0]
    terms = lax.all_to_all(
        rows.reshape(SITES, share, lanes), "col", 0, 0, axis_index_groups=across
    )
    y_cols, y_rows = place_last(gots, terms, result)
    return (y_rows, y_cols)


def solution(mesh):
    in_specs = (P(("row", "col"), None, None), P(("row", "col")), P(("row", "col")), P("col", None))
    out_specs = (P(("row", "col"), None), P("col", None))
    return jax.shard_map(
        on_device, mesh=mesh, in_specs=in_specs, out_specs=out_specs, check_vma=False
    )
```

```python
import functools

import jax
import jax.numpy as jnp
from jax import lax
from jax.experimental import pallas as pl
from jax.experimental.pallas import tpu as pltpu
from jax.sharding import PartitionSpec as P

RT_DEV = 2
CTD = 2
STEPS = 2
MIB = 1024 * 1024
PAD = 16
SITES = 16
PLANES = 4
BF16_MOST = 3.3895313892515355e38


def place_of(info, index, depth, width):
    slot = index // STEPS
    part = index % STEPS
    local_row = info[0, slot]
    local_col = info[1, slot]
    first = pl.multiple_of(local_row * width + part * depth, depth)
    rows = pl.ds(first, depth)
    cols = pl.ds(pl.multiple_of(local_col * width, width), width)
    piece = pl.ds(pl.multiple_of(part * depth, depth), depth)
    return slot, part, rows, cols, piece


def fetch_of(info, tiles_ref, held, sems):
    slots, width, _ = held.shape
    depth = width // STEPS

    def fetch(index):
        slot, part, rows, cols, piece = place_of(info, index, depth, width)
        return pltpu.make_async_copy(
            tiles_ref.at[slot, piece], held.at[slot, piece], sems.at[index]
        )

    return fetch


def row_kernel(info, tiles_ref, panel_ref, keep_ref, send_ref, total, held, sems):
    slots, width, _ = held.shape
    depth = width // STEPS
    fetch = fetch_of(info, tiles_ref, held, sems)
    for index in range(slots * STEPS):
        fetch(index).start()
    total[...] = jnp.zeros_like(total)

    @pl.loop(0, slots * STEPS)
    def _(index):
        slot, part, rows, cols, piece = place_of(info, index, depth, width)
        kind = info[2, slot]
        fetch(index).wait()

        @pl.when(kind == 1)
        def _():
            total[rows, :] += jnp.dot(
                held[slot, piece, :], panel_ref[cols, :], preferred_element_type=jnp.float32
            )

        @pl.when(kind == 2)
        def _():
            row_ids = lax.broadcasted_iota(jnp.int32, (depth, width), 0) + part * depth
            col_ids = lax.broadcasted_iota(jnp.int32, (depth, width), 1)
            tile = held[slot, piece, :].astype(jnp.float32)
            lower = jnp.where(row_ids >= col_ids, tile, 0.0).astype(jnp.bfloat16)
            strict = jnp.where(row_ids > col_ids, tile, 0.0).astype(jnp.bfloat16)
            total[rows, :] += jnp.dot(lower, panel_ref[cols, :], preferred_element_type=jnp.float32)
            own = pl.ds(pl.multiple_of(info[1, slot] * width + part * depth, depth), depth)
            whole = pl.ds(pl.multiple_of(info[0, slot] * width, width), width)
            total[whole, :] += lax.dot_general(
                panel_ref[own, :], strict, (((0,), (0,)), ((), ())),
                preferred_element_type=jnp.float32,
            ).T

    core = info[4, 0]
    depth_z = info[4, 1]
    share = total.shape[0] // (SITES * PLANES)
    for ref, which in ((keep_ref, core), (send_ref, 1 - core)):
        for step, chip in enumerate((depth_z, 1 - depth_z)):
            for site in range(SITES):
                source = pl.multiple_of((site * PLANES + chip * 2 + which) * share, share)
                target = (step * SITES + site) * share
                ref[target : target + share, :] = total[pl.ds(source, share), :]


def add_kernel(keep_ref, got_ref, mine_ref, send_ref):
    size = mine_ref.shape[0]
    mine_ref[...] = keep_ref[:size, :] + got_ref[:size, :]
    encode(keep_ref[size:, :] + got_ref[size:, :], send_ref)


def rows_kernel(mine_ref, got_ref, after_ref, token_ref, out_ref):
    del after_ref, token_ref
    out_ref[...] = mine_ref[...] + decode(got_ref)


def total_kernel(terms_ref, out_ref):
    total = terms_ref[0]
    for site in range(1, terms_ref.shape[0]):
        total += terms_ref[site]
    out_ref[...] = total


def block_rows(size):
    return min(128, size)


def encode(value, out_ref):
    size = value.shape[0]
    block = block_rows(size)
    lanes = value.shape[1]
    powers = []
    for start in range(0, size, block):
        part = value[start : start + block]
        most = jnp.max(jnp.abs(part), axis=0, keepdims=True)
        power = 15.0 - jnp.maximum(jnp.ceil(jnp.log2(most)), -126.0)
        half = jnp.floor(power * 0.5)
        scaled = part * jnp.exp2(half) * jnp.exp2(power - half)
        whole = jnp.clip(jnp.round(scaled), -32767.0, 32767.0)
        out_ref[start : start + block, :] = whole.astype(jnp.int32).astype(jnp.int16)
        powers.append(power)
    powers.append(jnp.zeros((PAD - len(powers), lanes), jnp.float32))
    tail = jnp.concatenate(powers, axis=0)
    out_ref[size:, :] = tail.astype(jnp.int32).astype(jnp.int16)


def decode(ref):
    size = ref.shape[0] - PAD
    block = block_rows(size)
    tail = ref[size:, :].astype(jnp.int32).astype(jnp.float32)
    parts = []
    for index in range(size // block):
        power = tail[index : index + 1]
        half = jnp.floor(power * 0.5)
        part = ref[index * block : (index + 1) * block, :].astype(jnp.int32).astype(jnp.float32)
        parts.append(part * jnp.exp2(-half) * jnp.exp2(half - power))
    return jnp.concatenate(parts, axis=0)


def fetch_kernel(tiles_ref, after_ref, held_ref, token_ref, sems):
    del after_ref
    slots, width, _ = held_ref.shape
    depth = width // STEPS
    copies = []
    for index in range(slots * STEPS):
        piece = pl.ds(index % STEPS * depth, depth)
        copies.append(
            pltpu.make_async_copy(
                tiles_ref.at[index // STEPS, piece],
                held_ref.at[index // STEPS, piece],
                sems.at[index],
            )
        )
    for copy in copies:
        copy.start()
    token_ref[...] = jnp.zeros_like(token_ref)
    for copy in copies:
        copy.wait()


def col_kernel(
    info, held, near_ref, far_ref, keep_ref, send0_ref, send1_ref, slab, total, result
):
    slots, width, _ = held.shape
    depth = width // STEPS
    total[...] = jnp.zeros_like(total)
    core = info[4, 0]
    for ref, tile in ((near_ref, core), (far_ref, 1 - core)):
        rows = pl.ds(pl.multiple_of(tile * width, width), width)
        slab[rows, :] = ref[...].reshape(width, slab.shape[1])

    @pl.loop(0, slots * STEPS)
    def _(index):
        slot, part, rows, cols, piece = place_of(info, index, depth, width)

        @pl.when(info[2, slot] == 1)
        def _():
            total[:, cols] += lax.dot_general(
                slab[rows, :], held[slot, piece, :], (((0,), (0,)), ((), ())),
                preferred_element_type=jnp.float32,
            )

    result[...] = total[...].T
    half = width // 2
    for index, send_ref in enumerate((send0_ref, send1_ref)):
        bit = info[3, index]
        mine = pl.multiple_of(index * width + bit * half, half)
        other = pl.multiple_of(index * width + (1 - bit) * half, half)
        keep_ref[index] = result[pl.ds(mine, half), :]
        encode(result[pl.ds(other, half), :], send_ref)


def first_kernel(index, keep_ref, got_ref, out_ref):
    encode(keep_ref[index] + decode(got_ref), out_ref)


def second_kernel(own_ref, got_ref, out_ref):
    encode(decode(own_ref) + decode(got_ref), out_ref)


def place_halves(far, half_refs, out_ref, held, sems):
    size = held.shape[1]
    row = lax.axis_index("row")
    high = row // 2
    copies = []
    for index, (half_ref, bit) in enumerate(zip(half_refs, ((row + high) % 2, high))):
        held[index] = decode(half_ref)
        side = 1 - bit if far else bit
        first = pl.multiple_of((index * 2 + side) * size, size)
        copy = pltpu.make_async_copy(
            held.at[index], out_ref.at[pl.ds(first, size)], sems.at[index]
        )
        copy.start()
        copies.append(copy)
    for copy in copies:
        copy.wait()


def own_kernel(half0_ref, half1_ref, out_ref, held, sems):
    place_halves(False, (half0_ref, half1_ref), out_ref, held, sems)


def last_kernel(half0_ref, half1_ref, result_ref, out_ref, held, sems):
    del result_ref
    place_halves(True, (half0_ref, half1_ref), out_ref, held, sems)


VMEM = pl.BlockSpec(memory_space=pltpu.VMEM)
SMEM = pl.BlockSpec(memory_space=pltpu.SMEM)
HBM = pl.BlockSpec(memory_space=pltpu.HBM)


def limit(size):
    return pltpu.CompilerParams(vmem_limit_bytes=size * MIB)


def small_call(kernel, outs, *args, scalars=0):
    return pl.pallas_call(
        kernel,
        in_specs=[SMEM] * scalars + [VMEM] * (len(args) - scalars),
        out_specs=[VMEM] * len(outs),
        out_shape=outs,
        compiler_params=limit(6),
    )(*args)


def place_scratch(size, lanes):
    return [pltpu.VMEM((2, size, lanes), jnp.float32), pltpu.SemaphoreType.DMA((2,))]


def place_own(owns):
    size, lanes = owns[0].shape[0] - PAD, owns[0].shape[1]
    return pl.pallas_call(
        own_kernel,
        in_specs=[VMEM, VMEM],
        out_specs=HBM,
        out_shape=floats(4 * size, lanes),
        scratch_shapes=place_scratch(size, lanes),
        compiler_params=limit(6),
    )(*owns)


def place_last(gots, result):
    size, lanes = gots[0].shape[0] - PAD, gots[0].shape[1]
    return pl.pallas_call(
        last_kernel,
        in_specs=[VMEM, VMEM, HBM],
        out_specs=HBM,
        out_shape=floats(4 * size, lanes),
        scratch_shapes=place_scratch(size, lanes),
        input_output_aliases={2: 0},
        compiler_params=limit(6),
    )(*gots, result)


def tile_cost(shape, lanes):
    slots, width, _ = shape
    return pl.CostEstimate(
        flops=2 * slots * width * width * lanes,
        bytes_accessed=2 * slots * width * width + 2 * MIB,
        transcendentals=0,
    )


def floats(*shape):
    return jax.ShapeDtypeStruct(shape, jnp.float32)


def coded(size, lanes):
    return jax.ShapeDtypeStruct((size + PAD, lanes), jnp.int16)


def tile_scratch(grm_tiles):
    return [
        pltpu.VMEM(grm_tiles.shape, grm_tiles.dtype),
        pltpu.SemaphoreType.DMA((grm_tiles.shape[0] * STEPS,)),
    ]


def row_products(info, grm_tiles, panel):
    slots, width, _ = grm_tiles.shape
    lanes = panel.shape[1]
    rows = RT_DEV * width
    return pl.pallas_call(
        row_kernel,
        in_specs=[SMEM, HBM, VMEM],
        out_specs=[VMEM, VMEM],
        out_shape=[floats(rows // 2, lanes), floats(rows // 2, lanes)],
        scratch_shapes=[pltpu.VMEM((rows, lanes), jnp.float32)] + tile_scratch(grm_tiles),
        compiler_params=limit(24),
        cost_estimate=tile_cost(grm_tiles.shape, lanes),
    )(info, grm_tiles, panel)


def fetch_tiles(grm_tiles, after):
    return pl.pallas_call(
        fetch_kernel,
        in_specs=[HBM, VMEM],
        out_specs=[VMEM, VMEM],
        out_shape=[pltpu.VMEM(grm_tiles.shape, grm_tiles.dtype), floats(8, 128)],
        scratch_shapes=[pltpu.SemaphoreType.DMA((grm_tiles.shape[0] * STEPS,))],
        compiler_params=limit(12),
    )(grm_tiles, after)


def col_products(info, grm_tiles, near, far):
    slots, width, _ = grm_tiles.shape
    lanes = near.shape[2]
    half = width // 2
    return pl.pallas_call(
        col_kernel,
        in_specs=[SMEM, VMEM, VMEM, VMEM],
        out_specs=[VMEM] * 3,
        out_shape=[floats(2, half, lanes), coded(half, lanes), coded(half, lanes)],
        scratch_shapes=[
            pltpu.VMEM((RT_DEV * width, lanes), near.dtype),
            pltpu.VMEM((lanes, CTD * width), jnp.float32),
            pltpu.VMEM((CTD * width, lanes), jnp.float32),
        ],
        compiler_params=limit(24),
        cost_estimate=tile_cost(grm_tiles.shape, lanes),
    )(info, grm_tiles, near, far)


def swap(value, axis, flip):
    return lax.ppermute(value, axis, [(k, k ^ flip) for k in range(lax.axis_size(axis))])


def sum_over_row(keep, sends):
    size, lanes = keep.shape[1:]
    outs = [coded(size, lanes)]
    flips = [(1, 3, 1), (3, 1, 3)]
    gots = [swap(send, "row", flip[0]) for send, flip in zip(sends, flips)]
    owns = [
        small_call(functools.partial(first_kernel, index), outs, keep, got)[0]
        for index, got in enumerate(gots)
    ]
    begun = owns[0]
    gots = [swap(own, "row", flip[1]) for own, flip in zip(owns, flips)]
    owns = [small_call(second_kernel, outs, own, got)[0] for own, got in zip(owns, gots)]
    gots = [swap(own, "row", flip[2]) for own, flip in zip(owns, flips)]
    return gots, place_own(owns), begun


def on_device(grm_tiles, tile_row, tile_col, panel):
    row_index = lax.axis_index("row")
    col_index = lax.axis_index("col")
    col_count = lax.axis_size("col")
    row_count = lax.axis_size("row")
    lanes = panel.shape[1]
    offset = CTD * col_count - RT_DEV * row_count
    base_row = row_index * RT_DEV
    base_col = col_index * CTD
    owners = [(offset + row * RT_DEV) // CTD for row in range(row_count)]

    local_row = tile_row - base_row
    local_col = jnp.maximum(tile_col - base_col, 0)
    kind = jnp.where(tile_col < 0, 0, jnp.where(tile_col == offset + tile_row, 2, 1))
    high = row_index // 2
    low = (row_index + high) % 2
    core = col_index % 2
    chip = col_index // 2 % 2
    root = (offset + base_row) // CTD
    chips = col_count // 2
    bits = jnp.stack([low, high, core, chip]).astype(jnp.int32)
    info = jnp.stack(
        [local_row, local_col, kind, jnp.pad(bits[:2], (0, 2)), jnp.pad(bits[2:4], (0, 2))]
    ).astype(jnp.int32)

    across = [[site * PLANES + plane for site in range(SITES)] for plane in range(PLANES)]
    tiles = pltpu.with_memory_space_constraint(grm_tiles, pltpu.HBM)
    one_core = [[chip * 2 + core for chip in range(chips)] for core in range(2)]
    size = panel.shape[0] // col_count
    pieces = lax.all_to_all(
        panel.reshape(col_count, size, lanes), "col", 0, 0,
        axis_index_groups=[one_core[0] + one_core[1]],
    )
    keep, send = row_products(info, tiles, panel)
    pieces, keep, send = lax.optimization_barrier((pieces, keep, send))
    half = keep.shape[0] // 2
    share = half // SITES
    mine, send_z = small_call(
        add_kernel, [floats(half, lanes), coded(half, lanes)], keep, swap(send, "col", 1)
    )
    place = root % 2 * chips + root // 2
    piece = lax.dynamic_index_in_dim(pieces, place, 0)
    packed = jnp.broadcast_to(piece, (chips, size, lanes))
    near = lax.all_to_all(packed, "col", 0, 0, axis_index_groups=one_core)
    got_z = swap(send_z, "col", 2)
    held, token = fetch_tiles(tiles, send_z)
    near, got_z, token = lax.optimization_barrier((near, got_z, token))
    far = swap(near, "col", 1)
    keep, *sends = col_products(info, held, near, far)
    gots, result, begun = sum_over_row(keep, sends)
    rows = small_call(rows_kernel, [floats(half, lanes)], mine, got_z, begun, token)[0]
    terms = lax.all_to_all(
        rows.reshape(SITES, share, lanes), "col", 0, 0, axis_index_groups=across
    )
    y_rows = small_call(total_kernel, [floats(share, lanes)], terms)[0]
    y_cols = place_last(gots, result)
    return (y_rows, y_cols)


def solution(mesh):
    in_specs = (P(("row", "col"), None, None), P(("row", "col")), P(("row", "col")), P("col", None))
    out_specs = (P(("row", "col"), None), P("col", None))
    return jax.shard_map(
        on_device, mesh=mesh, in_specs=in_specs, out_specs=out_specs, check_vma=False
    )
```

```python
import functools

import jax
import jax.numpy as jnp
from jax import lax
from jax.experimental import pallas as pl
from jax.experimental.pallas import tpu as pltpu
from jax.sharding import PartitionSpec as P

RT_DEV = 2
CTD = 2
STEPS = 2
MIB = 1024 * 1024
PAD = 16
SITES = 16
PLANES = 4
BF16_MOST = 3.3895313892515355e38


def place_of(info, index, depth, width):
    slot = index // STEPS
    part = index % STEPS
    local_row = info[0, slot]
    local_col = info[1, slot]
    first = pl.multiple_of(local_row * width + part * depth, depth)
    rows = pl.ds(first, depth)
    cols = pl.ds(pl.multiple_of(local_col * width, width), width)
    piece = pl.ds(pl.multiple_of(part * depth, depth), depth)
    return slot, part, rows, cols, piece


def fetch_of(info, tiles_ref, held, sems):
    slots, width, _ = held.shape
    depth = width // STEPS

    def fetch(index):
        slot, part, rows, cols, piece = place_of(info, index, depth, width)
        return pltpu.make_async_copy(
            tiles_ref.at[slot, piece], held.at[slot, piece], sems.at[index]
        )

    return fetch


def row_kernel(info, tiles_ref, panel_ref, keep_ref, send_ref, total, held, sems):
    slots, width, _ = held.shape
    depth = width // STEPS
    fetch = fetch_of(info, tiles_ref, held, sems)
    for index in range(slots * STEPS):
        fetch(index).start()
    total[...] = jnp.zeros_like(total)

    @pl.loop(0, slots * STEPS)
    def _(index):
        slot, part, rows, cols, piece = place_of(info, index, depth, width)
        kind = info[2, slot]
        fetch(index).wait()

        @pl.when(kind == 1)
        def _():
            total[rows, :] += jnp.dot(
                held[slot, piece, :], panel_ref[cols, :], preferred_element_type=jnp.float32
            )

        @pl.when(kind == 2)
        def _():
            row_ids = lax.broadcasted_iota(jnp.int32, (depth, width), 0) + part * depth
            col_ids = lax.broadcasted_iota(jnp.int32, (depth, width), 1)
            tile = held[slot, piece, :].astype(jnp.float32)
            lower = jnp.where(row_ids >= col_ids, tile, 0.0).astype(jnp.bfloat16)
            strict = jnp.where(row_ids > col_ids, tile, 0.0).astype(jnp.bfloat16)
            total[rows, :] += jnp.dot(lower, panel_ref[cols, :], preferred_element_type=jnp.float32)
            own = pl.ds(pl.multiple_of(info[1, slot] * width + part * depth, depth), depth)
            whole = pl.ds(pl.multiple_of(info[0, slot] * width, width), width)
            total[whole, :] += lax.dot_general(
                panel_ref[own, :], strict, (((0,), (0,)), ((), ())),
                preferred_element_type=jnp.float32,
            ).T

    core = info[4, 0]
    depth_z = info[4, 1]
    share = total.shape[0] // (SITES * PLANES)
    for ref, which in ((keep_ref, core), (send_ref, 1 - core)):
        for step, chip in enumerate((depth_z, 1 - depth_z)):
            for site in range(SITES):
                source = pl.multiple_of((site * PLANES + chip * 2 + which) * share, share)
                target = (step * SITES + site) * share
                ref[target : target + share, :] = total[pl.ds(source, share), :]


def add_kernel(keep_ref, got_ref, mine_ref, send_ref):
    size = mine_ref.shape[0]
    mine_ref[...] = keep_ref[:size, :] + got_ref[:size, :]
    encode(keep_ref[size:, :] + got_ref[size:, :], send_ref)


def rows_kernel(mine_ref, got_ref, after_ref, out_ref):
    del after_ref
    out_ref[...] = mine_ref[...] + decode(got_ref)


def total_kernel(terms_ref, out_ref):
    total = terms_ref[0]
    for site in range(1, terms_ref.shape[0]):
        total += terms_ref[site]
    out_ref[...] = total


def block_rows(size):
    return min(128, size)


def encode(value, out_ref):
    size = value.shape[0]
    block = block_rows(size)
    lanes = value.shape[1]
    powers = []
    for start in range(0, size, block):
        part = value[start : start + block]
        most = jnp.max(jnp.abs(part), axis=0, keepdims=True)
        power = 15.0 - jnp.maximum(jnp.ceil(jnp.log2(most)), -126.0)
        half = jnp.floor(power * 0.5)
        scaled = part * jnp.exp2(half) * jnp.exp2(power - half)
        whole = jnp.clip(jnp.round(scaled), -32767.0, 32767.0)
        out_ref[start : start + block, :] = whole.astype(jnp.int32).astype(jnp.int16)
        powers.append(power)
    powers.append(jnp.zeros((PAD - len(powers), lanes), jnp.float32))
    tail = jnp.concatenate(powers, axis=0)
    out_ref[size:, :] = tail.astype(jnp.int32).astype(jnp.int16)


def decode(ref):
    size = ref.shape[0] - PAD
    block = block_rows(size)
    tail = ref[size:, :].astype(jnp.int32).astype(jnp.float32)
    parts = []
    for index in range(size // block):
        power = tail[index : index + 1]
        half = jnp.floor(power * 0.5)
        part = ref[index * block : (index + 1) * block, :].astype(jnp.int32).astype(jnp.float32)
        parts.append(part * jnp.exp2(-half) * jnp.exp2(half - power))
    return jnp.concatenate(parts, axis=0)


def col_kernel(
    info, tiles_ref, near_ref, far_ref, keep_ref, send0_ref, send1_ref, slab, total, result, held, sems
):
    slots, width, _ = held.shape
    depth = width // STEPS
    fetch = fetch_of(info, tiles_ref, held, sems)
    for index in range(slots * STEPS):
        fetch(index).start()
    total[...] = jnp.zeros_like(total)
    core = info[4, 0]
    for ref, tile in ((near_ref, core), (far_ref, 1 - core)):
        rows = pl.ds(pl.multiple_of(tile * width, width), width)
        slab[rows, :] = ref[...].reshape(width, slab.shape[1])

    @pl.loop(0, slots * STEPS)
    def _(index):
        slot, part, rows, cols, piece = place_of(info, index, depth, width)
        fetch(index).wait()

        @pl.when(info[2, slot] == 1)
        def _():
            total[:, cols] += lax.dot_general(
                slab[rows, :], held[slot, piece, :], (((0,), (0,)), ((), ())),
                preferred_element_type=jnp.float32,
            )

    result[...] = total[...].T
    half = width // 2
    for index, send_ref in enumerate((send0_ref, send1_ref)):
        bit = info[3, index]
        mine = pl.multiple_of(index * width + bit * half, half)
        other = pl.multiple_of(index * width + (1 - bit) * half, half)
        keep_ref[index] = result[pl.ds(mine, half), :]
        encode(result[pl.ds(other, half), :], send_ref)


def first_kernel(index, keep_ref, got_ref, out_ref):
    encode(keep_ref[index] + decode(got_ref), out_ref)


def second_kernel(own_ref, got_ref, out_ref):
    encode(decode(own_ref) + decode(got_ref), out_ref)


def place_halves(far, half_refs, out_ref, held, sems):
    size = held.shape[1]
    row = lax.axis_index("row")
    high = row // 2
    copies = []
    for index, (half_ref, bit) in enumerate(zip(half_refs, ((row + high) % 2, high))):
        held[index] = decode(half_ref)
        side = 1 - bit if far else bit
        first = pl.multiple_of((index * 2 + side) * size, size)
        copy = pltpu.make_async_copy(
            held.at[index], out_ref.at[pl.ds(first, size)], sems.at[index]
        )
        copy.start()
        copies.append(copy)
    for copy in copies:
        copy.wait()


def own_kernel(half0_ref, half1_ref, out_ref, held, sems):
    place_halves(False, (half0_ref, half1_ref), out_ref, held, sems)


def last_kernel(half0_ref, half1_ref, result_ref, out_ref, held, sems):
    del result_ref
    place_halves(True, (half0_ref, half1_ref), out_ref, held, sems)


VMEM = pl.BlockSpec(memory_space=pltpu.VMEM)
SMEM = pl.BlockSpec(memory_space=pltpu.SMEM)
HBM = pl.BlockSpec(memory_space=pltpu.HBM)


def limit(size):
    return pltpu.CompilerParams(vmem_limit_bytes=size * MIB)


def small_call(kernel, outs, *args, scalars=0):
    return pl.pallas_call(
        kernel,
        in_specs=[SMEM] * scalars + [VMEM] * (len(args) - scalars),
        out_specs=[VMEM] * len(outs),
        out_shape=outs,
        compiler_params=limit(6),
    )(*args)


def place_scratch(size, lanes):
    return [pltpu.VMEM((2, size, lanes), jnp.float32), pltpu.SemaphoreType.DMA((2,))]


def place_own(owns):
    size, lanes = owns[0].shape[0] - PAD, owns[0].shape[1]
    return pl.pallas_call(
        own_kernel,
        in_specs=[VMEM, VMEM],
        out_specs=HBM,
        out_shape=floats(4 * size, lanes),
        scratch_shapes=place_scratch(size, lanes),
        compiler_params=limit(6),
    )(*owns)


def place_last(gots, result):
    size, lanes = gots[0].shape[0] - PAD, gots[0].shape[1]
    return pl.pallas_call(
        last_kernel,
        in_specs=[VMEM, VMEM, HBM],
        out_specs=HBM,
        out_shape=floats(4 * size, lanes),
        scratch_shapes=place_scratch(size, lanes),
        input_output_aliases={2: 0},
        compiler_params=limit(6),
    )(*gots, result)


def tile_cost(shape, lanes):
    slots, width, _ = shape
    return pl.CostEstimate(
        flops=2 * slots * width * width * lanes,
        bytes_accessed=2 * slots * width * width + 2 * MIB,
        transcendentals=0,
    )


def floats(*shape):
    return jax.ShapeDtypeStruct(shape, jnp.float32)


def coded(size, lanes):
    return jax.ShapeDtypeStruct((size + PAD, lanes), jnp.int16)


def tile_scratch(grm_tiles):
    return [
        pltpu.VMEM(grm_tiles.shape, grm_tiles.dtype),
        pltpu.SemaphoreType.DMA((grm_tiles.shape[0] * STEPS,)),
    ]


def row_products(info, grm_tiles, panel):
    slots, width, _ = grm_tiles.shape
    lanes = panel.shape[1]
    rows = RT_DEV * width
    return pl.pallas_call(
        row_kernel,
        in_specs=[SMEM, HBM, VMEM],
        out_specs=[VMEM, VMEM],
        out_shape=[floats(rows // 2, lanes), floats(rows // 2, lanes)],
        scratch_shapes=[pltpu.VMEM((rows, lanes), jnp.float32)] + tile_scratch(grm_tiles),
        compiler_params=limit(24),
        cost_estimate=tile_cost(grm_tiles.shape, lanes),
    )(info, grm_tiles, panel)


def col_products(info, grm_tiles, near, far):
    slots, width, _ = grm_tiles.shape
    lanes = near.shape[2]
    half = width // 2
    return pl.pallas_call(
        col_kernel,
        in_specs=[SMEM, HBM, VMEM, VMEM],
        out_specs=[VMEM] * 3,
        out_shape=[floats(2, half, lanes), coded(half, lanes), coded(half, lanes)],
        scratch_shapes=[
            pltpu.VMEM((RT_DEV * width, lanes), near.dtype),
            pltpu.VMEM((lanes, CTD * width), jnp.float32),
            pltpu.VMEM((CTD * width, lanes), jnp.float32),
        ]
        + tile_scratch(grm_tiles),
        compiler_params=limit(24),
        cost_estimate=tile_cost(grm_tiles.shape, lanes),
    )(info, grm_tiles, near, far)


def swap(value, axis, flip):
    return lax.ppermute(value, axis, [(k, k ^ flip) for k in range(lax.axis_size(axis))])


def sum_over_row(keep, sends):
    size, lanes = keep.shape[1:]
    outs = [coded(size, lanes)]
    flips = [(1, 3, 1), (3, 1, 3)]
    gots = [swap(send, "row", flip[0]) for send, flip in zip(sends, flips)]
    owns = [
        small_call(functools.partial(first_kernel, index), outs, keep, got)[0]
        for index, got in enumerate(gots)
    ]
    begun = owns[0]
    gots = [swap(own, "row", flip[1]) for own, flip in zip(owns, flips)]
    owns = [small_call(second_kernel, outs, own, got)[0] for own, got in zip(owns, gots)]
    gots = [swap(own, "row", flip[2]) for own, flip in zip(owns, flips)]
    return gots, place_own(owns), begun


def on_device(grm_tiles, tile_row, tile_col, panel):
    row_index = lax.axis_index("row")
    col_index = lax.axis_index("col")
    col_count = lax.axis_size("col")
    row_count = lax.axis_size("row")
    lanes = panel.shape[1]
    offset = CTD * col_count - RT_DEV * row_count
    base_row = row_index * RT_DEV
    base_col = col_index * CTD
    owners = [(offset + row * RT_DEV) // CTD for row in range(row_count)]

    local_row = tile_row - base_row
    local_col = jnp.maximum(tile_col - base_col, 0)
    kind = jnp.where(tile_col < 0, 0, jnp.where(tile_col == offset + tile_row, 2, 1))
    high = row_index // 2
    low = (row_index + high) % 2
    core = col_index % 2
    chip = col_index // 2 % 2
    root = (offset + base_row) // CTD
    chips = col_count // 2
    bits = jnp.stack([low, high, core, chip]).astype(jnp.int32)
    info = jnp.stack(
        [local_row, local_col, kind, jnp.pad(bits[:2], (0, 2)), jnp.pad(bits[2:4], (0, 2))]
    ).astype(jnp.int32)

    across = [[site * PLANES + plane for site in range(SITES)] for plane in range(PLANES)]
    tiles = pltpu.with_memory_space_constraint(grm_tiles, pltpu.HBM)
    one_core = [[chip * 2 + core for chip in range(chips)] for core in range(2)]
    size = panel.shape[0] // col_count
    pieces = lax.all_to_all(
        panel.reshape(col_count, size, lanes), "col", 0, 0,
        axis_index_groups=[one_core[0] + one_core[1]],
    )
    keep, send = row_products(info, tiles, panel)
    pieces, keep, send = lax.optimization_barrier((pieces, keep, send))
    half = keep.shape[0] // 2
    share = half // SITES
    mine, send_z = small_call(
        add_kernel, [floats(half, lanes), coded(half, lanes)], keep, swap(send, "col", 1)
    )
    place = root % 2 * chips + root // 2
    piece = lax.dynamic_index_in_dim(pieces, place, 0)
    packed = jnp.broadcast_to(piece, (chips, size, lanes))
    near = lax.all_to_all(packed, "col", 0, 0, axis_index_groups=one_core)
    near, got_z = lax.optimization_barrier((near, swap(send_z, "col", 2)))
    far = swap(near, "col", 1)
    keep, *sends = col_products(info, tiles, near, far)
    gots, result, begun = sum_over_row(keep, sends)
    rows = small_call(rows_kernel, [floats(half, lanes)], mine, got_z, begun)[0]
    terms = lax.all_to_all(
        rows.reshape(SITES, share, lanes), "col", 0, 0, axis_index_groups=across
    )
    y_rows = small_call(total_kernel, [floats(share, lanes)], terms)[0]
    y_cols = place_last(gots, result)
    return (y_rows, y_cols)


def solution(mesh):
    in_specs = (P(("row", "col"), None, None), P(("row", "col")), P(("row", "col")), P("col", None))
    out_specs = (P(("row", "col"), None), P("col", None))
    return jax.shard_map(
        on_device, mesh=mesh, in_specs=in_specs, out_specs=out_specs, check_vma=False
    )
```

```python
import functools

import jax
import jax.numpy as jnp
from jax import lax
from jax.experimental import pallas as pl
from jax.experimental.pallas import tpu as pltpu
from jax.sharding import PartitionSpec as P

RT_DEV = 2
CTD = 2
STEPS = 2
MIB = 1024 * 1024
PAD = 16
SITES = 16
PLANES = 4
BF16_MOST = 3.3895313892515355e38


def place_of(info, index, depth, width):
    slot = index // STEPS
    part = index % STEPS
    local_row = info[0, slot]
    local_col = info[1, slot]
    first = pl.multiple_of(local_row * width + part * depth, depth)
    rows = pl.ds(first, depth)
    cols = pl.ds(pl.multiple_of(local_col * width, width), width)
    piece = pl.ds(pl.multiple_of(part * depth, depth), depth)
    return slot, part, rows, cols, piece


def fetch_of(info, tiles_ref, held, sems):
    slots, width, _ = held.shape
    depth = width // STEPS

    def fetch(index):
        slot, part, rows, cols, piece = place_of(info, index, depth, width)
        return pltpu.make_async_copy(
            tiles_ref.at[slot, piece], held.at[slot, piece], sems.at[index]
        )

    return fetch


def row_kernel(info, tiles_ref, panel_ref, keep_ref, send_ref, total, held, sems):
    slots, width, _ = held.shape
    depth = width // STEPS
    fetch = fetch_of(info, tiles_ref, held, sems)
    for index in range(slots * STEPS):
        fetch(index).start()
    total[...] = jnp.zeros_like(total)

    @pl.loop(0, slots * STEPS)
    def _(index):
        slot, part, rows, cols, piece = place_of(info, index, depth, width)
        kind = info[2, slot]
        fetch(index).wait()

        @pl.when(kind == 1)
        def _():
            total[rows, :] += jnp.dot(
                held[slot, piece, :], panel_ref[cols, :], preferred_element_type=jnp.float32
            )

        @pl.when(kind == 2)
        def _():
            row_ids = lax.broadcasted_iota(jnp.int32, (depth, width), 0) + part * depth
            col_ids = lax.broadcasted_iota(jnp.int32, (depth, width), 1)
            tile = held[slot, piece, :].astype(jnp.float32)
            lower = jnp.where(row_ids >= col_ids, tile, 0.0).astype(jnp.bfloat16)
            strict = jnp.where(row_ids > col_ids, tile, 0.0).astype(jnp.bfloat16)
            total[rows, :] += jnp.dot(lower, panel_ref[cols, :], preferred_element_type=jnp.float32)
            own = pl.ds(pl.multiple_of(info[1, slot] * width + part * depth, depth), depth)
            whole = pl.ds(pl.multiple_of(info[0, slot] * width, width), width)
            total[whole, :] += lax.dot_general(
                panel_ref[own, :], strict, (((0,), (0,)), ((), ())),
                preferred_element_type=jnp.float32,
            ).T

    core = info[4, 0]
    depth_z = info[4, 1]
    share = total.shape[0] // (SITES * PLANES)
    for ref, which in ((keep_ref, core), (send_ref, 1 - core)):
        for step, chip in enumerate((depth_z, 1 - depth_z)):
            for site in range(SITES):
                source = pl.multiple_of((site * PLANES + chip * 2 + which) * share, share)
                target = (step * SITES + site) * share
                ref[target : target + share, :] = total[pl.ds(source, share), :]


def add_kernel(keep_ref, got_ref, mine_ref, send_ref):
    size = mine_ref.shape[0]
    mine_ref[...] = keep_ref[:size, :] + got_ref[:size, :]
    encode(keep_ref[size:, :] + got_ref[size:, :], send_ref)


def rows_kernel(mine_ref, got_ref, after_ref, out_ref):
    del after_ref
    out_ref[...] = mine_ref[...] + decode(got_ref)


def total_kernel(terms_ref, out_ref):
    total = terms_ref[0]
    for site in range(1, terms_ref.shape[0]):
        total += terms_ref[site]
    out_ref[...] = total


def block_rows(size):
    return min(128, size)


def encode(value, out_ref):
    size = value.shape[0]
    block = block_rows(size)
    lanes = value.shape[1]
    powers = []
    for start in range(0, size, block):
        part = value[start : start + block]
        most = jnp.max(jnp.abs(part), axis=0, keepdims=True)
        power = 15.0 - jnp.maximum(jnp.ceil(jnp.log2(most)), -126.0)
        half = jnp.floor(power * 0.5)
        scaled = part * jnp.exp2(half) * jnp.exp2(power - half)
        whole = jnp.clip(jnp.round(scaled), -32767.0, 32767.0)
        out_ref[start : start + block, :] = whole.astype(jnp.int32).astype(jnp.int16)
        powers.append(power)
    powers.append(jnp.zeros((PAD - len(powers), lanes), jnp.float32))
    tail = jnp.concatenate(powers, axis=0)
    out_ref[size:, :] = tail.astype(jnp.int32).astype(jnp.int16)


def decode(ref):
    size = ref.shape[0] - PAD
    block = block_rows(size)
    tail = ref[size:, :].astype(jnp.int32).astype(jnp.float32)
    parts = []
    for index in range(size // block):
        power = tail[index : index + 1]
        half = jnp.floor(power * 0.5)
        part = ref[index * block : (index + 1) * block, :].astype(jnp.int32).astype(jnp.float32)
        parts.append(part * jnp.exp2(-half) * jnp.exp2(half - power))
    return jnp.concatenate(parts, axis=0)


def col_kernel(
    info_ref, tiles_ref, near_ref, far_ref, keep_ref, send0_ref, send1_ref, slab, total, result, held, sems, info, info_sem
):
    slots, width, _ = held.shape
    depth = width // STEPS
    info_copy = pltpu.make_async_copy(info_ref, info, info_sem)
    info_copy.start()
    fetch = fetch_of(info, tiles_ref, held, sems)
    for index in range(slots * STEPS):
        slot, piece = index // STEPS, pl.ds(index % STEPS * depth, depth)
        pltpu.make_async_copy(
            tiles_ref.at[slot, piece], held.at[slot, piece], sems.at[index]
        ).start()
    total[...] = jnp.zeros_like(total)
    core = lax.axis_index("col") % 2
    for ref, tile in ((near_ref, core), (far_ref, 1 - core)):
        rows = pl.ds(pl.multiple_of(tile * width, width), width)
        slab[rows, :] = ref[...].reshape(width, slab.shape[1])

    info_copy.wait()

    @pl.loop(0, slots * STEPS)
    def _(index):
        slot, part, rows, cols, piece = place_of(info, index, depth, width)
        fetch(index).wait()

        @pl.when(info[2, slot] == 1)
        def _():
            total[:, cols] += lax.dot_general(
                slab[rows, :], held[slot, piece, :], (((0,), (0,)), ((), ())),
                preferred_element_type=jnp.float32,
            )

    result[...] = total[...].T
    half = width // 2
    for index, send_ref in enumerate((send0_ref, send1_ref)):
        bit = info[3, index]
        mine = pl.multiple_of(index * width + bit * half, half)
        other = pl.multiple_of(index * width + (1 - bit) * half, half)
        keep_ref[index] = result[pl.ds(mine, half), :]
        encode(result[pl.ds(other, half), :], send_ref)


def first_kernel(index, keep_ref, got_ref, out_ref):
    encode(keep_ref[index] + decode(got_ref), out_ref)


def second_kernel(own_ref, got_ref, out_ref):
    encode(decode(own_ref) + decode(got_ref), out_ref)


def place_halves(far, half_refs, out_ref, held, sems):
    size = held.shape[1]
    row = lax.axis_index("row")
    high = row // 2
    copies = []
    for index, (half_ref, bit) in enumerate(zip(half_refs, ((row + high) % 2, high))):
        held[index] = decode(half_ref)
        side = 1 - bit if far else bit
        first = pl.multiple_of((index * 2 + side) * size, size)
        copy = pltpu.make_async_copy(
            held.at[index], out_ref.at[pl.ds(first, size)], sems.at[index]
        )
        copy.start()
        copies.append(copy)
    for copy in copies:
        copy.wait()


def own_kernel(half0_ref, half1_ref, out_ref, held, sems):
    place_halves(False, (half0_ref, half1_ref), out_ref, held, sems)


def last_kernel(half0_ref, half1_ref, result_ref, out_ref, held, sems):
    del result_ref
    place_halves(True, (half0_ref, half1_ref), out_ref, held, sems)


VMEM = pl.BlockSpec(memory_space=pltpu.VMEM)
SMEM = pl.BlockSpec(memory_space=pltpu.SMEM)
HBM = pl.BlockSpec(memory_space=pltpu.HBM)


def limit(size):
    return pltpu.CompilerParams(vmem_limit_bytes=size * MIB)


def small_call(kernel, outs, *args, scalars=0):
    return pl.pallas_call(
        kernel,
        in_specs=[SMEM] * scalars + [VMEM] * (len(args) - scalars),
        out_specs=[VMEM] * len(outs),
        out_shape=outs,
        compiler_params=limit(6),
    )(*args)


def place_scratch(size, lanes):
    return [pltpu.VMEM((2, size, lanes), jnp.float32), pltpu.SemaphoreType.DMA((2,))]


def place_own(owns):
    size, lanes = owns[0].shape[0] - PAD, owns[0].shape[1]
    return pl.pallas_call(
        own_kernel,
        in_specs=[VMEM, VMEM],
        out_specs=HBM,
        out_shape=floats(4 * size, lanes),
        scratch_shapes=place_scratch(size, lanes),
        compiler_params=limit(6),
    )(*owns)


def place_last(gots, result):
    size, lanes = gots[0].shape[0] - PAD, gots[0].shape[1]
    return pl.pallas_call(
        last_kernel,
        in_specs=[VMEM, VMEM, HBM],
        out_specs=HBM,
        out_shape=floats(4 * size, lanes),
        scratch_shapes=place_scratch(size, lanes),
        input_output_aliases={2: 0},
        compiler_params=limit(6),
    )(*gots, result)


def tile_cost(shape, lanes):
    slots, width, _ = shape
    return pl.CostEstimate(
        flops=2 * slots * width * width * lanes,
        bytes_accessed=2 * slots * width * width + 2 * MIB,
        transcendentals=0,
    )


def floats(*shape):
    return jax.ShapeDtypeStruct(shape, jnp.float32)


def coded(size, lanes):
    return jax.ShapeDtypeStruct((size + PAD, lanes), jnp.int16)


def tile_scratch(grm_tiles):
    return [
        pltpu.VMEM(grm_tiles.shape, grm_tiles.dtype),
        pltpu.SemaphoreType.DMA((grm_tiles.shape[0] * STEPS,)),
    ]


def row_products(info, grm_tiles, panel):
    slots, width, _ = grm_tiles.shape
    lanes = panel.shape[1]
    rows = RT_DEV * width
    return pl.pallas_call(
        row_kernel,
        in_specs=[SMEM, HBM, VMEM],
        out_specs=[VMEM, VMEM],
        out_shape=[floats(rows // 2, lanes), floats(rows // 2, lanes)],
        scratch_shapes=[pltpu.VMEM((rows, lanes), jnp.float32)] + tile_scratch(grm_tiles),
        compiler_params=limit(24),
        cost_estimate=tile_cost(grm_tiles.shape, lanes),
    )(info, grm_tiles, panel)


def col_products(info, grm_tiles, near, far):
    slots, width, _ = grm_tiles.shape
    lanes = near.shape[2]
    half = width // 2
    return pl.pallas_call(
        col_kernel,
        in_specs=[pl.BlockSpec(memory_space=pl.ANY), HBM, VMEM, VMEM],
        out_specs=[VMEM] * 3,
        out_shape=[floats(2, half, lanes), coded(half, lanes), coded(half, lanes)],
        scratch_shapes=[
            pltpu.VMEM((RT_DEV * width, lanes), near.dtype),
            pltpu.VMEM((lanes, CTD * width), jnp.float32),
            pltpu.VMEM((CTD * width, lanes), jnp.float32),
        ]
        + tile_scratch(grm_tiles)
        + [pltpu.SMEM(info.shape, info.dtype), pltpu.SemaphoreType.DMA],
        compiler_params=limit(24),
        cost_estimate=tile_cost(grm_tiles.shape, lanes),
    )(info, grm_tiles, near, far)


def swap(value, axis, flip):
    return lax.ppermute(value, axis, [(k, k ^ flip) for k in range(lax.axis_size(axis))])


def sum_over_row(keep, sends):
    size, lanes = keep.shape[1:]
    outs = [coded(size, lanes)]
    flips = [(1, 3, 1), (3, 1, 3)]
    gots = [swap(send, "row", flip[0]) for send, flip in zip(sends, flips)]
    owns = [
        small_call(functools.partial(first_kernel, index), outs, keep, got)[0]
        for index, got in enumerate(gots)
    ]
    begun = owns[0]
    gots = [swap(own, "row", flip[1]) for own, flip in zip(owns, flips)]
    owns = [small_call(second_kernel, outs, own, got)[0] for own, got in zip(owns, gots)]
    gots = [swap(own, "row", flip[2]) for own, flip in zip(owns, flips)]
    return gots, place_own(owns), begun


def on_device(grm_tiles, tile_row, tile_col, panel):
    row_index = lax.axis_index("row")
    col_index = lax.axis_index("col")
    col_count = lax.axis_size("col")
    row_count = lax.axis_size("row")
    lanes = panel.shape[1]
    offset = CTD * col_count - RT_DEV * row_count
    base_row = row_index * RT_DEV
    base_col = col_index * CTD
    owners = [(offset + row * RT_DEV) // CTD for row in range(row_count)]

    local_row = tile_row - base_row
    local_col = jnp.maximum(tile_col - base_col, 0)
    kind = jnp.where(tile_col < 0, 0, jnp.where(tile_col == offset + tile_row, 2, 1))
    high = row_index // 2
    low = (row_index + high) % 2
    core = col_index % 2
    chip = col_index // 2 % 2
    root = (offset + base_row) // CTD
    chips = col_count // 2
    bits = jnp.stack([low, high, core, chip]).astype(jnp.int32)
    info = jnp.stack(
        [local_row, local_col, kind, jnp.pad(bits[:2], (0, 2)), jnp.pad(bits[2:4], (0, 2))]
    ).astype(jnp.int32)

    across = [[site * PLANES + plane for site in range(SITES)] for plane in range(PLANES)]
    tiles = pltpu.with_memory_space_constraint(grm_tiles, pltpu.HBM)
    one_core = [[chip * 2 + core for chip in range(chips)] for core in range(2)]
    size = panel.shape[0] // col_count
    pieces = lax.all_to_all(
        panel.reshape(col_count, size, lanes), "col", 0, 0,
        axis_index_groups=[one_core[0] + one_core[1]],
    )
    keep, send = row_products(info, tiles, panel)
    pieces, keep, send = lax.optimization_barrier((pieces, keep, send))
    half = keep.shape[0] // 2
    share = half // SITES
    mine, send_z = small_call(
        add_kernel, [floats(half, lanes), coded(half, lanes)], keep, swap(send, "col", 1)
    )
    place = root % 2 * chips + root // 2
    piece = lax.dynamic_index_in_dim(pieces, place, 0)
    packed = jnp.broadcast_to(piece, (chips, size, lanes))
    near = lax.all_to_all(packed, "col", 0, 0, axis_index_groups=one_core)
    near, got_z = lax.optimization_barrier((near, swap(send_z, "col", 2)))
    far = swap(near, "col", 1)
    keep, *sends = col_products(info, tiles, near, far)
    gots, result, begun = sum_over_row(keep, sends)
    rows = small_call(rows_kernel, [floats(half, lanes)], mine, got_z, begun)[0]
    terms = lax.all_to_all(
        rows.reshape(SITES, share, lanes), "col", 0, 0, axis_index_groups=across
    )
    y_rows = small_call(total_kernel, [floats(share, lanes)], terms)[0]
    y_cols = place_last(gots, result)
    return (y_rows, y_cols)


def solution(mesh):
    in_specs = (P(("row", "col"), None, None), P(("row", "col")), P(("row", "col")), P("col", None))
    out_specs = (P(("row", "col"), None), P("col", None))
    return jax.shard_map(
        on_device, mesh=mesh, in_specs=in_specs, out_specs=out_specs, check_vma=False
    )
```
